32 devices in a mesh: groups: 2 (over x), feat: 8 (over z, y), store: 2 (over core).
Axes of the slice: x: 2, y: 2, z: 4, core: 2. Of those that a mesh axis runs over, the one named last changes fastest.
Arguments:
- activations: bfloat16 [6144, 8192], P(('groups', 'store'), 'feat'), parts along dimension 0, may hold values from -6 to 6
- output_grads: bfloat16 [6144, 8192], P(('groups', 'store'), 'feat'), parts along dimension 0, may hold values from -6 to 6
- input_basis: bfloat16 [8192, 64], P('feat'), may hold values from -0.0625 to 0.0625
- grad_basis: bfloat16 [8192, 64], P('feat'), may hold values from -0.0625 to 0.0625
- lengths: int32 [96], P(('groups', 'store')), parts along dimension 0, may hold values from 1 to 64, as said below
- stored_grads: bfloat16 [24576, 4096], P(('groups', 'feat', 'store')), parts along dimension 0, may hold values from -0.09375 to 0.09375
Outputs:
- scores: float32 [96, 12288], P('groups', ('feat', 'store')), parts along dimension 0
The draws below stay inside these ranges and needn't reach their ends.
There are 2 independent parts, one for each index of `groups`. The reference program is written for one: setup_inputs(seed, part) draws one part's arguments, and reference() takes and returns one part's arrays. A program takes and returns all parts, laid end to end along the dimension named above; an argument that names none is the same for every part. Nothing has to cross between parts.
Inputs may be any that keep to these rules, and one draw needn't show every extreme that they name: `lengths`: every document has at least one live token; some document fills all 64 slots and some has one.
All inputs are finite; a program needn't handle non-finite values.
Results may differ from the reference program's by a relative error of at most 0.0029.
Values may be sent and summed in bfloat16 or wider, within the bound.
A program may use at most 64 MiB of HBM per device.

```python
import jax
import jax.numpy as jnp
from jax import lax

D = 8192
R = 64
TOKDOC = 64
DOCS = 48
TOKENS = 3072
STORE_ROWS = 12288


def draw_lengths(key, part):
    values = jax.random.randint(key, (DOCS,), 1, TOKDOC + 1).astype(jnp.int32)
    first = jax.random.randint(jax.random.fold_in(key, 7), (), 0, DOCS)
    second = (first + 1 + jax.random.randint(jax.random.fold_in(key, 11), (), 0, DOCS - 1)) % DOCS
    values = values.at[first].set(TOKDOC)
    values = values.at[second].set(1)
    return values.astype(jnp.int32)


def with_spikes(array, rng, source, target, shards_of, factor):
    def block_of(dim):
        return (jnp.arange(array.shape[dim]) // (array.shape[dim] // shards_of)).reshape((-1,) + (1,) * (array.ndim - 1 - dim))

    near = jax.random.permutation(rng, shards_of)[block_of(target)]
    far = (block_of(target) + shards_of // 2) % shards_of
    return jnp.where((block_of(source) == near) | (block_of(source) == far), factor * array, array)


def block_scale(rng, extent, cuts, smallest, top_value):
    gain, own = 1.0, jax.random.fold_in(rng, 6)
    for dim, parts in cuts:
        steps = jnp.exp(jax.random.uniform(jax.random.fold_in(own, dim), (parts,), jnp.float32, smallest / len(cuts), top_value / len(cuts)))
        gain = gain * jnp.repeat(steps, extent[dim] // parts).reshape([-1 if axis == dim else 1 for axis in range(len(extent))])
    return gain


def normal_values(rng, dims, spread, reach, cuts=(), kind=jnp.bfloat16):
    level = block_scale(rng, dims, cuts, -0.22, 0.18) if cuts else 1.0
    result = jax.random.normal(rng, dims, jnp.float32) * spread * level
    return jnp.minimum(jnp.maximum(result, -reach), reach).astype(kind)


def heavy_noise(own_key, extent, spread, bound, pieces, heavy, dtype=jnp.bfloat16):
    result = spread * jax.random.normal(own_key, extent, jnp.float32)
    if pieces:
        result = result * block_scale(own_key, extent, pieces, -0.22, 0.18)
    return jnp.clip(with_spikes(result, jax.random.fold_in(own_key, 3), *heavy), -bound, bound).astype(dtype)


def setup_inputs(seed: int = 0, part: int = 0) -> dict:
    seeds = jax.random.split(jax.random.key(seed), 7)
    part_keys = jax.random.split(jax.random.fold_in(seeds[6], part), 7)
    activations = heavy_noise(part_keys[0], (TOKENS, D), 1.0, 6.0, ((0, 2), (1, 8)), (1, 0, 8, 2.0))
    output_grads = normal_values(part_keys[1], (TOKENS, D), 1.0, 6.0, ((0, 2), (1, 8)))
    input_basis = normal_values(seeds[2], (D, R), D ** -0.5, 0.0625, ((0, 8),))
    grad_basis = normal_values(seeds[3], (D, R), D ** -0.5, 0.0625, ((0, 8),))
    lengths = draw_lengths(jax.random.fold_in(jax.random.fold_in(seeds[6], part), 71), part)
    stored_grads = normal_values(part_keys[5], (STORE_ROWS, R * R), (R * R) ** -0.5, 0.09375, ((0, 16),))
    return dict(activations=activations, output_grads=output_grads, input_basis=input_basis, grad_basis=grad_basis, lengths=lengths, stored_grads=stored_grads)


def document_grads(summed, doc_lengths):
    count = doc_lengths.shape[0]
    blocks = summed.reshape(count, TOKDOC, 2 * R)
    position = lax.broadcasted_iota(jnp.int32, (count, TOKDOC, 1), 1)
    keeper = (position < doc_lengths[:, None, None]).astype(jnp.float32)
    grad_side = blocks[:, :, :R] * keeper
    input_side = blocks[:, :, R:]
    outer = jnp.einsum("ntr,nts->nrs", grad_side, input_side, precision=lax.Precision.HIGHEST)
    scaled = outer / doc_lengths.astype(jnp.float32)[:, None, None]
    return scaled.reshape(count, R * R).astype(jnp.bfloat16)


def reference(activations, output_grads, input_basis, grad_basis, lengths, stored_grads):
    grad_proj = jnp.dot(output_grads, grad_basis, preferred_element_type=jnp.float32)
    input_proj = jnp.dot(activations, input_basis, preferred_element_type=jnp.float32)
    projected = jnp.concatenate([grad_proj, input_proj], axis=1)
    queries = document_grads(projected, lengths)
    return lax.dot_general(queries, stored_grads, (((1,), (1,)), ((), ())), preferred_element_type=jnp.float32)
```

```python
import functools

import jax
import jax.numpy as jnp
from jax import lax
from jax.experimental import pallas as pl
from jax.experimental.pallas import tpu as pltpu
from jax.sharding import PartitionSpec as P

MESH = pl.DeviceIdType.MESH
PAIR = 2
HALVES = 2
LANES = 128


def remote(src, dst, send_sem, recv_sem, target):
    return pltpu.make_async_remote_copy(
        src_ref=src, dst_ref=dst, send_sem=send_sem, recv_sem=recv_sem, device_id=target, device_id_type=MESH
    )


def kernel(
    feat, stores, slots_per_doc,
    acts, grads, in_basis, grad_basis, lengths, stored, scores,
    acts_v, grads_v, in_basis_v, grad_basis_v, stored_v, partial,
    pair_out, pair_in, line_out, line_in, gathered, wide, queries,
    acts_sem, grads_sem, basis_sem, stored_sem,
    pair_send, pair_recv, line_send, line_recv, all_send, all_recv, core_send, core_recv,
):
    line = feat // PAIR
    block = acts_v.shape[1] // PAIR
    docs = block // slots_per_doc
    rank = in_basis.shape[1]
    pairs = rank * rank // LANES
    part_rows = pairs // HALVES
    order = list(range(1, line)) + [0]

    me = lax.axis_index("feat")
    core = lax.axis_index("store")
    my_line, my_pair = me // PAIR, lax.rem(me, PAIR)
    other = 1 - my_pair
    twin = my_line * PAIR + other

    basis_loads = [
        pltpu.make_async_copy(in_basis, in_basis_v, basis_sem.at[0]),
        pltpu.make_async_copy(grad_basis, grad_basis_v, basis_sem.at[1]),
    ]
    for load in basis_loads:
        load.start()
    loads = {}
    for step in order:
        spot = lax.rem(my_line + step, line)
        rows = pl.ds(pl.multiple_of(spot * (PAIR * block), PAIR * block), PAIR * block)
        loads[step] = [
            pltpu.make_async_copy(acts.at[rows], acts_v.at[step], acts_sem.at[step]),
            pltpu.make_async_copy(grads.at[rows], grads_v.at[step], grads_sem.at[step]),
        ]
        for load in loads[step]:
            load.start()

    barrier = pltpu.get_barrier_semaphore()
    for shift in range(1, feat):
        pl.semaphore_signal(barrier, inc=1, device_id={"feat": lax.rem(me + shift, feat)}, device_id_type=MESH)
    for shift in range(1, stores):
        pl.semaphore_signal(barrier, inc=1, device_id={"store": lax.rem(core + shift, stores)}, device_id_type=MESH)

    row = lax.broadcasted_iota(jnp.int32, (rank, LANES), 0)
    lane = lax.broadcasted_iota(jnp.int32, (rank, LANES), 1)
    grad_place = (lane == (row % 2) * (rank // 2) + row // 2).astype(jnp.bfloat16)
    in_place = (lane == row + rank).astype(jnp.bfloat16)
    for load in basis_loads:
        load.wait()
    in_wide = jnp.dot(in_basis_v[...], in_place, preferred_element_type=jnp.float32).astype(jnp.bfloat16)
    grad_wide = jnp.dot(grad_basis_v[...], grad_place, preferred_element_type=jnp.float32).astype(jnp.bfloat16)

    pair_copies = {}
    for index, step in enumerate(order):
        for load in loads[step]:
            load.wait()
        partial[step] = jnp.dot(acts_v[step], in_wide, preferred_element_type=jnp.float32) + jnp.dot(
            grads_v[step], grad_wide, preferred_element_type=jnp.float32
        )
        theirs = pl.ds(pl.multiple_of(other * block, block), block)
        pair_out[step] = partial[step, theirs, :]
        if index == 0:
            pl.semaphore_wait(barrier, feat - 1 + stores - 1)
        pair_copies[step] = remote(
            pair_out.at[step], pair_in.at[step], pair_send.at[step], pair_recv.at[step], {"feat": twin}
        )
        pair_copies[step].start()

    half = stored.shape[1] // HALVES
    stored_loads = []
    for part in range(HALVES):
        columns = pl.ds(part * half, half)
        load = pltpu.make_async_copy(stored.at[:, columns], stored_v.at[part], stored_sem.at[part])
        load.start()
        stored_loads.append(load)

    mine = pl.ds(pl.multiple_of(my_pair * block, block), block)
    line_copies = {}
    total = None
    for step in order:
        pair_copies[step].wait_recv()
        both = partial[step, mine, :] + pair_in[step]
        if step == 0:
            total = both
        else:
            line_out[step] = both
            spot = lax.rem(my_line + step, line)
            line_copies[step] = remote(
                line_out.at[step], line_in.at[step], line_send.at[step], line_recv.at[step],
                {"feat": spot * PAIR + my_pair},
            )
            line_copies[step].start()
    for step in order[:-1]:
        line_copies[step].wait_recv()
        total = total + line_in[step]

    position = lax.broadcasted_iota(jnp.int32, (slots_per_doc, rank), 0)
    left = lax.broadcasted_iota(jnp.int32, (slots_per_doc, LANES), 1) < rank
    slot = core * feat + me
    for doc in range(docs):
        length = lengths[me * docs + doc]
        rows = total[doc * slots_per_doc:(doc + 1) * slots_per_doc]
        grad_side = jnp.where(position < length, rows[:, :rank], 0.0)
        in_side = jnp.where(left, pltpu.roll(rows, rank, 1), rows)
        outer = lax.dot_general(
            grad_side, in_side, (((0,), (0,)), ((), ())),
            precision=lax.Precision.HIGHEST, preferred_element_type=jnp.float32,
        )
        query = jnp.where(left[:pairs], outer[:pairs], outer[pairs:]) / length.astype(jnp.float32)
        query = query.astype(jnp.bfloat16)
        for part in range(HALVES):
            gathered[part, slot, pl.ds(doc * part_rows, part_rows), :] = query[part * part_rows:(part + 1) * part_rows]

    sent = []
    for part in range(HALVES):
        own = gathered.at[part, slot]
        for shift in range(1, stores):
            sent.append(remote(
                own, own, core_send.at[part, shift, 0], core_recv.at[part, shift, 0],
                {"store": lax.rem(core + shift, stores)},
            ))
            sent[-1].start()
        for shift in range(1, feat):
            sent.append(remote(
                own, own, all_send.at[part, shift], all_recv.at[part, shift], {"feat": lax.rem(me + shift, feat)}
            ))
            sent[-1].start()

    wide_rows = wide.shape[0]
    all_docs = queries.shape[0]
    tile = 256
    for part in range(HALVES):
        for shift in range(1, feat):
            source = core * feat + lax.rem(me + feat - shift, feat)
            there = gathered.at[part, source]
            remote(
                there, there, all_send.at[part, shift], all_recv.at[part, shift], {"feat": lax.rem(me + shift, feat)}
            ).wait_recv()
            for hop in range(1, stores):
                sent.append(remote(
                    there, there, core_send.at[part, hop, shift], core_recv.at[part, hop, shift],
                    {"store": lax.rem(core + hop, stores)},
                ))
                sent[-1].start()
        for hop in range(1, stores):
            from_core = lax.rem(core + stores - hop, stores)
            for shift in range(feat):
                there = gathered.at[part, from_core * feat + lax.rem(me + feat - shift, feat)]
                remote(
                    there, there, core_send.at[part, hop, shift], core_recv.at[part, hop, shift],
                    {"store": lax.rem(core + hop, stores)},
                ).wait_recv()
        wide[...] = gathered[part].reshape(wide_rows, LANES).astype(jnp.float32)
        for pair in range(part_rows):
            queries[:, pair * LANES:(pair + 1) * LANES] = wide[pl.ds(pair, all_docs, part_rows), :].astype(jnp.bfloat16)
        stored_loads[part].wait()
        for start in range(0, stored.shape[0], tile):
            product = lax.dot_general(
                queries[...], stored_v[part, start:start + tile, :], (((1,), (1,)), ((), ())),
                preferred_element_type=jnp.float32,
            )
            if part == 0:
                scores[:, start:start + tile] = product
            else:
                scores[:, start:start + tile] += product

    for step in order:
        pair_copies[step].wait_send()
        if step:
            line_copies[step].wait_send()
    for copy in sent:
        copy.wait_send()


def per_device(feat, stores, activations, output_grads, input_basis, grad_basis, lengths, stored_grads):
    tokens, features = activations.shape
    slots_per_doc = tokens // lengths.shape[0]
    rank = input_basis.shape[1]
    rows, depth = stored_grads.shape
    docs = lengths.shape[0] * stores
    line = feat // PAIR
    block = tokens // feat
    part_rows = rank * rank // LANES // HALVES
    share = block // slots_per_doc * part_rows
    bf16, f32 = jnp.bfloat16, jnp.float32
    dma = pltpu.SemaphoreType.DMA
    anywhere = pl.BlockSpec(memory_space=pl.ANY)
    return pl.pallas_call(
        functools.partial(kernel, feat, stores, slots_per_doc),
        out_shape=jax.ShapeDtypeStruct((docs, rows), f32),
        in_specs=[anywhere] * 4 + [pl.BlockSpec(memory_space=pltpu.SMEM), anywhere],
        out_specs=pl.BlockSpec(memory_space=pltpu.VMEM),
        scratch_shapes=[
            pltpu.VMEM((line, PAIR * block, features), bf16),
            pltpu.VMEM((line, PAIR * block, features), bf16),
            pltpu.VMEM((features, rank), bf16),
            pltpu.VMEM((features, rank), bf16),
            pltpu.VMEM((HALVES, rows, depth // HALVES), bf16),
            pltpu.VMEM((line, PAIR * block, LANES), f32),
            pltpu.VMEM((line, block, LANES), f32),
            pltpu.VMEM((line, block, LANES), f32),
            pltpu.VMEM((line, block, LANES), f32),
            pltpu.VMEM((line, block, LANES), f32),
            pltpu.VMEM((HALVES, stores * feat, share, LANES), bf16),
            pltpu.VMEM((docs * part_rows, LANES), f32),
            pltpu.VMEM((docs, depth // HALVES), bf16),
            dma((line,)), dma((line,)), dma((2,)), dma((HALVES,)),
            dma((line,)), dma((line,)), dma((line,)), dma((line,)),
            dma((HALVES, feat)), dma((HALVES, feat)),
            dma((HALVES, stores, feat)), dma((HALVES, stores, feat)),
        ],
        compiler_params=pltpu.CompilerParams(
            collective_id=0, has_side_effects=True, vmem_limit_bytes=56 * 1024 * 1024
        ),
        cost_estimate=pl.CostEstimate(
            flops=4 * tokens * features * rank + 2 * docs * rows * depth,
            bytes_accessed=4 * tokens * features + 2 * rows * depth + 4 * docs * rows,
            transcendentals=0,
        ),
    )(activations, output_grads, input_basis, grad_basis, lengths, stored_grads)


def solution(mesh):
    placed = (
        P(("groups", "store"), "feat"),
        P(("groups", "store"), "feat"),
        P("feat", None),
        P("feat", None),
        P(("groups", "store")),
        P(("groups", "feat", "store"), None),
    )
    return jax.shard_map(
        functools.partial(per_device, mesh.shape["feat"], mesh.shape["store"]),
        mesh=mesh,
        in_specs=placed,
        out_specs=P("groups", ("feat", "store")),
        check_vma=False,
    )
```

```python
import functools

import jax
import jax.numpy as jnp
from jax import lax
from jax.experimental import pallas as pl
from jax.experimental.pallas import tpu as pltpu
from jax.sharding import PartitionSpec as P

MESH = pl.DeviceIdType.MESH
PAIR = 2
HALVES = 2
LANES = 128
HEADER = 16


def remote(src, dst, send_sem, recv_sem, target):
    return pltpu.make_async_remote_copy(
        src_ref=src, dst_ref=dst, send_sem=send_sem, recv_sem=recv_sem, device_id=target, device_id_type=MESH
    )


def encode(ref, values):
    block = values.shape[0]
    top = jnp.max(jnp.abs(values), axis=0, keepdims=True)
    power = 14.0 - jnp.floor(jnp.log2(jnp.maximum(top, 1e-30)))
    scaled = jnp.clip(jnp.round(values * jnp.exp2(power)), -32767.0, 32767.0)
    ref[:block] = scaled.astype(jnp.int32).astype(jnp.int16)
    ref[block:] = jnp.broadcast_to(power, (ref.shape[0] - block, LANES)).astype(jnp.int32).astype(jnp.int16)


def decode(ref, block):
    values = ref[:block].astype(jnp.int32).astype(jnp.float32)
    power = ref[block:].astype(jnp.int32).astype(jnp.float32)[:1]
    return values * jnp.exp2(-power)


def kernel(
    feat, stores, slots_per_doc,
    acts, grads, in_basis, grad_basis, lengths, stored, scores,
    acts_v, grads_v, in_basis_v, grad_basis_v, stored_v, partial,
    pair_out, pair_in, line_out, line_in, gathered, wide, queries,
    acts_sem, grads_sem, basis_sem, stored_sem,
    pair_send, pair_recv, line_send, line_recv, all_send, all_recv, core_send, core_recv,
):
    line = feat // PAIR
    block = acts_v.shape[1] // PAIR
    docs = block // slots_per_doc
    rank = in_basis.shape[0]
    pairs = rank * rank // LANES
    part_rows = pairs // HALVES
    order = list(range(1, line)) + [0]

    me = lax.axis_index("feat")
    core = lax.axis_index("store")
    my_line, my_pair = me // PAIR, lax.rem(me, PAIR)
    other = 1 - my_pair
    twin = my_line * PAIR + other

    basis_loads = [
        pltpu.make_async_copy(in_basis, in_basis_v, basis_sem.at[0]),
        pltpu.make_async_copy(grad_basis, grad_basis_v, basis_sem.at[1]),
    ]
    for load in basis_loads:
        load.start()
    loads = {}
    for step in order:
        spot = lax.rem(my_line + step, line)
        rows = pl.ds(pl.multiple_of(spot * (PAIR * block), PAIR * block), PAIR * block)
        loads[step] = [
            pltpu.make_async_copy(acts.at[rows], acts_v.at[step], acts_sem.at[step]),
            pltpu.make_async_copy(grads.at[rows], grads_v.at[step], grads_sem.at[step]),
        ]
        for load in loads[step]:
            load.start()

    barrier = pltpu.get_barrier_semaphore()
    for shift in range(1, feat):
        pl.semaphore_signal(barrier, inc=1, device_id={"feat": lax.rem(me + shift, feat)}, device_id_type=MESH)
    for shift in range(1, stores):
        pl.semaphore_signal(barrier, inc=1, device_id={"store": lax.rem(core + shift, stores)}, device_id_type=MESH)

    row = lax.broadcasted_iota(jnp.int32, (rank, LANES), 0)
    lane = lax.broadcasted_iota(jnp.int32, (rank, LANES), 1)
    grad_place = (lane == (row % 2) * (rank // 2) + row // 2).astype(jnp.bfloat16)
    in_place = (lane == row + rank).astype(jnp.bfloat16)
    for load in basis_loads:
        load.wait()
    over_rank = (((0,), (0,)), ((), ()))
    in_wide = lax.dot_general(in_basis_v[...], in_place, over_rank, preferred_element_type=jnp.float32)
    grad_wide = lax.dot_general(grad_basis_v[...], grad_place, over_rank, preferred_element_type=jnp.float32)
    in_wide, grad_wide = in_wide.astype(jnp.bfloat16), grad_wide.astype(jnp.bfloat16)

    pair_copies = {}
    for index, step in enumerate(order):
        for load in loads[step]:
            load.wait()
        partial[step] = jnp.dot(acts_v[step], in_wide, preferred_element_type=jnp.float32) + jnp.dot(
            grads_v[step], grad_wide, preferred_element_type=jnp.float32
        )
        theirs = pl.ds(pl.multiple_of(other * block, block), block)
        encode(pair_out.at[step], partial[step, theirs, :])
        if index == 0:
            pl.semaphore_wait(barrier, feat - 1 + stores - 1)
        pair_copies[step] = remote(
            pair_out.at[step], pair_in.at[step], pair_send.at[step], pair_recv.at[step], {"feat": twin}
        )
        pair_copies[step].start()

    half = stored.shape[1] // HALVES
    stored_loads = []
    for part in range(HALVES):
        columns = pl.ds(part * half, half)
        load = pltpu.make_async_copy(stored.at[:, columns], stored_v.at[part], stored_sem.at[part])
        load.start()
        stored_loads.append(load)

    mine = pl.ds(pl.multiple_of(my_pair * block, block), block)
    line_copies = {}
    total = None
    for step in order:
        pair_copies[step].wait_recv()
        both = partial[step, mine, :] + decode(pair_in.at[step], block)
        if step == 0:
            total = both
        else:
            encode(line_out.at[step], both)
            spot = lax.rem(my_line + step, line)
            line_copies[step] = remote(
                line_out.at[step], line_in.at[step], line_send.at[step], line_recv.at[step],
                {"feat": spot * PAIR + my_pair},
            )
            line_copies[step].start()
    for step in order[:-1]:
        line_copies[step].wait_recv()
        total = total + decode(line_in.at[step], block)

    position = lax.broadcasted_iota(jnp.int32, (slots_per_doc, rank), 0)
    left = lax.broadcasted_iota(jnp.int32, (slots_per_doc, LANES), 1) < rank
    slot = core * feat + me
    for doc in range(docs):
        length = lengths[me * docs + doc]
        rows = total[doc * slots_per_doc:(doc + 1) * slots_per_doc]
        grad_side = jnp.where(position < length, rows[:, :rank], 0.0)
        in_side = jnp.where(left, pltpu.roll(rows, rank, 1), rows)
        outer = lax.dot_general(
            grad_side, in_side, (((0,), (0,)), ((), ())),
            precision=lax.Precision.HIGHEST, preferred_element_type=jnp.float32,
        )
        query = jnp.where(left[:pairs], outer[:pairs], outer[pairs:]) / length.astype(jnp.float32)
        query = query.astype(jnp.bfloat16)
        for part in range(HALVES):
            gathered[part, slot, pl.ds(doc * part_rows, part_rows), :] = query[part * part_rows:(part + 1) * part_rows]

    sent = []
    for part in range(HALVES):
        own = gathered.at[part, slot]
        for shift in range(1, stores):
            sent.append(remote(
                own, own, core_send.at[part, shift, 0], core_recv.at[part, shift, 0],
                {"store": lax.rem(core + shift, stores)},
            ))
            sent[-1].start()
        for shift in range(1, feat):
            sent.append(remote(
                own, own, all_send.at[part, shift], all_recv.at[part, shift], {"feat": lax.rem(me + shift, feat)}
            ))
            sent[-1].start()

    wide_rows = wide.shape[0]
    all_docs = queries.shape[0]
    tile = 256
    for part in range(HALVES):
        for shift in range(1, feat):
            source = core * feat + lax.rem(me + feat - shift, feat)
            there = gathered.at[part, source]
            remote(
                there, there, all_send.at[part, shift], all_recv.at[part, shift], {"feat": lax.rem(me + shift, feat)}
            ).wait_recv()
            for hop in range(1, stores):
                sent.append(remote(
                    there, there, core_send.at[part, hop, shift], core_recv.at[part, hop, shift],
                    {"store": lax.rem(core + hop, stores)},
                ))
                sent[-1].start()
        for hop in range(1, stores):
            from_core = lax.rem(core + stores - hop, stores)
            for shift in range(feat):
                there = gathered.at[part, from_core * feat + lax.rem(me + feat - shift, feat)]
                remote(
                    there, there, core_send.at[part, hop, shift], core_recv.at[part, hop, shift],
                    {"store": lax.rem(core + hop, stores)},
                ).wait_recv()
        wide[...] = gathered[part].reshape(wide_rows, LANES).astype(jnp.float32)
        for pair in range(part_rows):
            queries[:, pair * LANES:(pair + 1) * LANES] = wide[pl.ds(pair, all_docs, part_rows), :].astype(jnp.bfloat16)
        stored_loads[part].wait()
        for start in range(0, stored.shape[0], tile):
            product = lax.dot_general(
                queries[...], stored_v[part, start:start + tile, :], (((1,), (1,)), ((), ())),
                preferred_element_type=jnp.float32,
            )
            if part == 0:
                scores[:, start:start + tile] = product
            else:
                scores[:, start:start + tile] += product

    for step in order:
        pair_copies[step].wait_send()
        if step:
            line_copies[step].wait_send()
    for copy in sent:
        copy.wait_send()


def per_device(feat, stores, activations, output_grads, input_basis, grad_basis, lengths, stored_grads):
    tokens, features = activations.shape
    slots_per_doc = tokens // lengths.shape[0]
    rank = input_basis.shape[1]
    rows, depth = stored_grads.shape
    docs = lengths.shape[0] * stores
    line = feat // PAIR
    block = tokens // feat
    part_rows = rank * rank // LANES // HALVES
    share = block // slots_per_doc * part_rows
    bf16, f32 = jnp.bfloat16, jnp.float32
    dma = pltpu.SemaphoreType.DMA
    anywhere = pl.BlockSpec(memory_space=pl.ANY)
    return pl.pallas_call(
        functools.partial(kernel, feat, stores, slots_per_doc),
        out_shape=jax.ShapeDtypeStruct((docs, rows), f32),
        in_specs=[anywhere] * 4 + [pl.BlockSpec(memory_space=pltpu.SMEM), anywhere],
        out_specs=pl.BlockSpec(memory_space=pltpu.VMEM),
        scratch_shapes=[
            pltpu.VMEM((line, PAIR * block, features), bf16),
            pltpu.VMEM((line, PAIR * block, features), bf16),
            pltpu.VMEM((rank, features), bf16),
            pltpu.VMEM((rank, features), bf16),
            pltpu.VMEM((HALVES, rows, depth // HALVES), bf16),
            pltpu.VMEM((line, PAIR * block, LANES), f32),
            pltpu.VMEM((line, block + HEADER, LANES), jnp.int16),
            pltpu.VMEM((line, block + HEADER, LANES), jnp.int16),
            pltpu.VMEM((line, block + HEADER, LANES), jnp.int16),
            pltpu.VMEM((line, block + HEADER, LANES), jnp.int16),
            pltpu.VMEM((HALVES, stores * feat, share, LANES), bf16),
            pltpu.VMEM((docs * part_rows, LANES), f32),
            pltpu.VMEM((docs, depth // HALVES), bf16),
            dma((line,)), dma((line,)), dma((2,)), dma((HALVES,)),
            dma((line,)), dma((line,)), dma((line,)), dma((line,)),
            dma((HALVES, feat)), dma((HALVES, feat)),
            dma((HALVES, stores, feat)), dma((HALVES, stores, feat)),
        ],
        compiler_params=pltpu.CompilerParams(
            collective_id=0, has_side_effects=True, vmem_limit_bytes=56 * 1024 * 1024
        ),
        cost_estimate=pl.CostEstimate(
            flops=4 * tokens * features * rank + 2 * docs * rows * depth,
            bytes_accessed=4 * tokens * features + 2 * rows * depth + 4 * docs * rows,
            transcendentals=0,
        ),
    )(activations, output_grads, input_basis.T, grad_basis.T, lengths, stored_grads)


def solution(mesh):
    placed = (
        P(("groups", "store"), "feat"),
        P(("groups", "store"), "feat"),
        P("feat", None),
        P("feat", None),
        P(("groups", "store")),
        P(("groups", "feat", "store"), None),
    )
    return jax.shard_map(
        functools.partial(per_device, mesh.shape["feat"], mesh.shape["store"]),
        mesh=mesh,
        in_specs=placed,
        out_specs=P("groups", ("feat", "store")),
        check_vma=False,
    )
```

```python
import functools

import jax
import jax.numpy as jnp
from jax import lax
from jax.experimental import pallas as pl
from jax.experimental.pallas import tpu as pltpu
from jax.sharding import PartitionSpec as P

MESH = pl.DeviceIdType.MESH
PAIR = 2
HALVES = 2
LANES = 128
HEADER = 16


def remote(src, dst, send_sem, recv_sem, target):
    return pltpu.make_async_remote_copy(
        src_ref=src, dst_ref=dst, send_sem=send_sem, recv_sem=recv_sem, device_id=target, device_id_type=MESH
    )


def encode(ref, values):
    block = values.shape[0]
    top = jnp.max(jnp.abs(values), axis=0, keepdims=True)
    power = 14.0 - jnp.floor(jnp.log2(jnp.maximum(top, 1e-30)))
    scaled = jnp.clip(jnp.round(values * jnp.exp2(power)), -32767.0, 32767.0)
    ref[:block] = scaled.astype(jnp.int32).astype(jnp.int16)
    ref[block:] = jnp.broadcast_to(power, (ref.shape[0] - block, LANES)).astype(jnp.int32).astype(jnp.int16)


def decode(ref, block):
    values = ref[:block].astype(jnp.int32).astype(jnp.float32)
    power = ref[block:].astype(jnp.int32).astype(jnp.float32)[:1]
    return values * jnp.exp2(-power)


def kernel(
    feat, stores, slots_per_doc,
    acts, grads, in_basis, grad_basis, lengths, stored, scores,
    acts_v, grads_v, in_basis_v, grad_basis_v, stored_v, partial,
    pair_out, pair_in, line_out, line_in, gathered, wide, queries,
    acts_sem, grads_sem, basis_sem, stored_sem,
    pair_send, pair_recv, line_send, line_recv, all_send, all_recv, twin_send, twin_recv, core_send, core_recv,
):
    line = feat // PAIR
    block = acts_v.shape[1] // PAIR
    docs = block // slots_per_doc
    rank = in_basis.shape[0]
    pairs = rank * rank // LANES
    part_rows = pairs // HALVES
    order = list(range(1, line)) + [0]

    me = lax.axis_index("feat")
    core = lax.axis_index("store")
    my_line, my_pair = me // PAIR, lax.rem(me, PAIR)
    other = 1 - my_pair
    twin = my_line * PAIR + other

    basis_loads = [
        pltpu.make_async_copy(in_basis, in_basis_v, basis_sem.at[0]),
        pltpu.make_async_copy(grad_basis, grad_basis_v, basis_sem.at[1]),
    ]
    for load in basis_loads:
        load.start()
    loads = {}
    for step in order:
        spot = lax.rem(my_line + step, line)
        rows = pl.ds(pl.multiple_of(spot * (PAIR * block), PAIR * block), PAIR * block)
        loads[step] = [
            pltpu.make_async_copy(acts.at[rows], acts_v.at[step], acts_sem.at[step]),
            pltpu.make_async_copy(grads.at[rows], grads_v.at[step], grads_sem.at[step]),
        ]
        for load in loads[step]:
            load.start()

    barrier = pltpu.get_barrier_semaphore()
    partners = [{"feat": twin}]
    partners += [{"feat": lax.rem(my_line + shift, line) * PAIR + my_pair} for shift in range(1, line)]
    partners += [{"store": lax.rem(core + shift, stores)} for shift in range(1, stores)]
    for partner in partners:
        pl.semaphore_signal(barrier, inc=1, device_id=partner, device_id_type=MESH)

    row = lax.broadcasted_iota(jnp.int32, (rank, LANES), 0)
    lane = lax.broadcasted_iota(jnp.int32, (rank, LANES), 1)
    grad_place = (lane == (row % 2) * (rank // 2) + row // 2).astype(jnp.bfloat16)
    in_place = (lane == row + rank).astype(jnp.bfloat16)
    for load in basis_loads:
        load.wait()
    over_rank = (((0,), (0,)), ((), ()))
    in_wide = lax.dot_general(in_basis_v[...], in_place, over_rank, preferred_element_type=jnp.float32)
    grad_wide = lax.dot_general(grad_basis_v[...], grad_place, over_rank, preferred_element_type=jnp.float32)
    in_wide, grad_wide = in_wide.astype(jnp.bfloat16), grad_wide.astype(jnp.bfloat16)

    pair_copies = {}
    for index, step in enumerate(order):
        for load in loads[step]:
            load.wait()
        partial[step] = jnp.dot(acts_v[step], in_wide, preferred_element_type=jnp.float32) + jnp.dot(
            grads_v[step], grad_wide, preferred_element_type=jnp.float32
        )
        theirs = pl.ds(pl.multiple_of(other * block, block), block)
        encode(pair_out.at[step], partial[step, theirs, :])
        if index == 0:
            pl.semaphore_wait(barrier, len(partners))
        pair_copies[step] = remote(
            pair_out.at[step], pair_in.at[step], pair_send.at[step], pair_recv.at[step], {"feat": twin}
        )
        pair_copies[step].start()

    half = stored.shape[1] // HALVES
    stored_loads = []
    for part in range(HALVES):
        columns = pl.ds(part * half, half)
        load = pltpu.make_async_copy(stored.at[:, columns], stored_v.at[part], stored_sem.at[part])
        load.start()
        stored_loads.append(load)

    mine = pl.ds(pl.multiple_of(my_pair * block, block), block)
    line_copies = {}
    total = None
    for step in order:
        pair_copies[step].wait_recv()
        both = partial[step, mine, :] + decode(pair_in.at[step], block)
        if step == 0:
            total = both
        else:
            encode(line_out.at[step], both)
            spot = lax.rem(my_line + step, line)
            line_copies[step] = remote(
                line_out.at[step], line_in.at[step], line_send.at[step], line_recv.at[step],
                {"feat": spot * PAIR + my_pair},
            )
            line_copies[step].start()
    for step in order[:-1]:
        line_copies[step].wait_recv()
        total = total + decode(line_in.at[step], block)

    position = lax.broadcasted_iota(jnp.int32, (slots_per_doc, rank), 0)
    left = lax.broadcasted_iota(jnp.int32, (slots_per_doc, LANES), 1) < rank
    for doc in range(docs):
        length = lengths[me * docs + doc]
        rows = total[doc * slots_per_doc:(doc + 1) * slots_per_doc]
        grad_side = jnp.where(position < length, rows[:, :rank], 0.0)
        in_side = jnp.where(left, pltpu.roll(rows, rank, 1), rows)
        outer = lax.dot_general(
            grad_side, in_side, (((0,), (0,)), ((), ())),
            precision=lax.Precision.HIGHEST, preferred_element_type=jnp.float32,
        )
        query = jnp.where(left[:pairs], outer[:pairs], outer[pairs:]) / length.astype(jnp.float32)
        query = query.astype(jnp.bfloat16)
        for part in range(HALVES):
            gathered[part, core, my_pair, my_line, pl.ds(doc * part_rows, part_rows), :] = query[part * part_rows:(part + 1) * part_rows]

    sent = []

    def send(*copy):
        sent.append(remote(*copy))
        sent[-1].start()

    def share(part, source, hop):
        for shift in range(1, stores):
            send(
                gathered.at[part, core, source], gathered.at[part, core, source],
                core_send.at[part, shift, hop], core_recv.at[part, shift, hop],
                {"store": lax.rem(core + shift, stores)},
            )

    def to_twin(part, spot, shift):
        there = gathered.at[part, core, my_pair, spot]
        send(there, there, twin_send.at[part, shift], twin_recv.at[part, shift], {"feat": twin})

    def along_line(part):
        for shift in range(1, line):
            source = lax.rem(my_line + line - shift, line)
            there = gathered.at[part, core, my_pair, source]
            remote(
                there, there, all_send.at[part, shift], all_recv.at[part, shift], {"feat": twin}
            ).wait_recv()
            to_twin(part, source, shift)
        share(part, my_pair, 0)

    def from_twin(part):
        for shift in range(line):
            there = gathered.at[part, core, other, lax.rem(my_line + line - shift, line)]
            remote(
                there, there, twin_send.at[part, shift], twin_recv.at[part, shift], {"feat": twin}
            ).wait_recv()
        share(part, other, 1)

    def from_cores(part):
        for shift in range(1, stores):
            for hop, source in enumerate((my_pair, other)):
                there = gathered.at[part, lax.rem(core + stores - shift, stores), source]
                remote(
                    there, there, core_send.at[part, shift, hop], core_recv.at[part, shift, hop],
                    {"store": lax.rem(core + shift, stores)},
                ).wait_recv()

    for part in range(HALVES):
        own = gathered.at[part, core, my_pair, my_line]
        for shift in range(1, line):
            send(
                own, own, all_send.at[part, shift], all_recv.at[part, shift],
                {"feat": lax.rem(my_line + shift, line) * PAIR + my_pair},
            )
        to_twin(part, my_line, 0)
    along_line(0)
    from_twin(0)

    wide_rows = wide.shape[0]
    all_docs = queries.shape[0]
    tile = 256
    for part in range(HALVES):
        if part + 1 < HALVES:
            along_line(part + 1)
        from_cores(part)
        wide[...] = jnp.concatenate(
            [gathered[part, c, f % PAIR, f // PAIR] for c in range(stores) for f in range(feat)]
        ).astype(jnp.float32)
        for pair in range(part_rows):
            queries[:, pair * LANES:(pair + 1) * LANES] = wide[pl.ds(pair, all_docs, part_rows), :].astype(jnp.bfloat16)
        stored_loads[part].wait()
        for start in range(0, stored.shape[0], tile):
            product = lax.dot_general(
                queries[...], stored_v[part, start:start + tile, :], (((1,), (1,)), ((), ())),
                preferred_element_type=jnp.float32,
            )
            if part == 0:
                scores[:, start:start + tile] = product
            else:
                scores[:, start:start + tile] += product
        if part + 1 < HALVES:
            from_twin(part + 1)

    for step in order:
        pair_copies[step].wait_send()
        if step:
            line_copies[step].wait_send()
    for copy in sent:
        copy.wait_send()


def per_device(feat, stores, activations, output_grads, input_basis, grad_basis, lengths, stored_grads):
    tokens, features = activations.shape
    slots_per_doc = tokens // lengths.shape[0]
    rank = input_basis.shape[1]
    rows, depth = stored_grads.shape
    docs = lengths.shape[0] * stores
    line = feat // PAIR
    block = tokens // feat
    part_rows = rank * rank // LANES // HALVES
    share = block // slots_per_doc * part_rows
    bf16, f32 = jnp.bfloat16, jnp.float32
    dma = pltpu.SemaphoreType.DMA
    anywhere = pl.BlockSpec(memory_space=pl.ANY)
    return pl.pallas_call(
        functools.partial(kernel, feat, stores, slots_per_doc),
        out_shape=jax.ShapeDtypeStruct((docs, rows), f32),
        in_specs=[anywhere] * 4 + [pl.BlockSpec(memory_space=pltpu.SMEM), anywhere],
        out_specs=pl.BlockSpec(memory_space=pltpu.VMEM),
        scratch_shapes=[
            pltpu.VMEM((line, PAIR * block, features), bf16),
            pltpu.VMEM((line, PAIR * block, features), bf16),
            pltpu.VMEM((rank, features), bf16),
            pltpu.VMEM((rank, features), bf16),
            pltpu.VMEM((HALVES, rows, depth // HALVES), bf16),
            pltpu.VMEM((line, PAIR * block, LANES), f32),
            pltpu.VMEM((line, block + HEADER, LANES), jnp.int16),
            pltpu.VMEM((line, block + HEADER, LANES), jnp.int16),
            pltpu.VMEM((line, block + HEADER, LANES), jnp.int16),
            pltpu.VMEM((line, block + HEADER, LANES), jnp.int16),
            pltpu.VMEM((HALVES, stores, PAIR, line, share, LANES), bf16),
            pltpu.VMEM((docs * part_rows, LANES), f32),
            pltpu.VMEM((docs, depth // HALVES), bf16),
            dma((line,)), dma((line,)), dma((2,)), dma((HALVES,)),
            dma((line,)), dma((line,)), dma((line,)), dma((line,)),
            dma((HALVES, line)), dma((HALVES, line)), dma((HALVES, line)), dma((HALVES, line)),
            dma((HALVES, stores, PAIR)), dma((HALVES, stores, PAIR)),
        ],
        compiler_params=pltpu.CompilerParams(
            collective_id=0, has_side_effects=True, vmem_limit_bytes=56 * 1024 * 1024
        ),
        cost_estimate=pl.CostEstimate(
            flops=4 * tokens * features * rank + 2 * docs * rows * depth,
            bytes_accessed=4 * tokens * features + 2 * rows * depth + 4 * docs * rows,
            transcendentals=0,
        ),
    )(activations, output_grads, input_basis.T, grad_basis.T, lengths, stored_grads)


def solution(mesh):
    placed = (
        P(("groups", "store"), "feat"),
        P(("groups", "store"), "feat"),
        P("feat", None),
        P("feat", None),
        P(("groups", "store")),
        P(("groups", "feat", "store"), None),
    )
    return jax.shard_map(
        functools.partial(per_device, mesh.shape["feat"], mesh.shape["store"]),
        mesh=mesh,
        in_specs=placed,
        out_specs=P("groups", ("feat", "store")),
        check_vma=False,
    )
```

```python
import functools

import jax
import jax.numpy as jnp
from jax import lax
from jax.experimental import pallas as pl
from jax.experimental.pallas import tpu as pltpu
from jax.sharding import PartitionSpec as P

MESH = pl.DeviceIdType.MESH
PAIR = 2
HALVES = 2
LANES = 128
HEADER = 16


def remote(src, dst, send_sem, recv_sem, target):
    return pltpu.make_async_remote_copy(
        src_ref=src, dst_ref=dst, send_sem=send_sem, recv_sem=recv_sem, device_id=target, device_id_type=MESH
    )


def encode(ref, values):
    block = values.shape[0]
    top = jnp.max(jnp.abs(values), axis=0, keepdims=True)
    power = 14.0 - jnp.floor(jnp.log2(jnp.maximum(top, 1e-30)))
    scaled = jnp.clip(jnp.round(values * jnp.exp2(power)), -32767.0, 32767.0)
    ref[:block] = scaled.astype(jnp.int32).astype(jnp.int16)
    ref[block:] = jnp.broadcast_to(power, (ref.shape[0] - block, LANES)).astype(jnp.int32).astype(jnp.int16)


def decode(ref, block):
    values = ref[:block].astype(jnp.int32).astype(jnp.float32)
    power = ref[block:].astype(jnp.int32).astype(jnp.float32)[:1]
    return values * jnp.exp2(-power)


def kernel(
    feat, stores, slots_per_doc,
    acts, grads, in_basis, grad_basis, lengths, stored, scores,
    acts_v, grads_v, in_basis_v, grad_basis_v, stored_v, partial,
    pair_out, pair_in, line_out, line_in, gathered, wide, queries, sums,
    acts_sem, grads_sem, basis_sem, stored_sem,
    pair_send, pair_recv, line_send, line_recv, all_send, all_recv, core_send, core_recv,
):
    line = feat // PAIR
    block = acts_v.shape[1] // PAIR
    docs = block // slots_per_doc
    rank = in_basis.shape[0]
    pairs = rank * rank // LANES
    part_rows = pairs // HALVES
    order = list(range(1, line)) + [0]

    me = lax.axis_index("feat")
    core = lax.axis_index("store")
    my_line, my_pair = me // PAIR, lax.rem(me, PAIR)
    other = 1 - my_pair
    twin = my_line * PAIR + other

    basis_loads = [
        pltpu.make_async_copy(in_basis, in_basis_v, basis_sem.at[0]),
        pltpu.make_async_copy(grad_basis, grad_basis_v, basis_sem.at[1]),
    ]
    for load in basis_loads:
        load.start()
    loads = {}
    for step in order:
        spot = lax.rem(my_line + step, line)
        rows = pl.ds(pl.multiple_of(spot * (PAIR * block), PAIR * block), PAIR * block)
        loads[step] = [
            pltpu.make_async_copy(acts.at[rows], acts_v.at[step], acts_sem.at[step]),
            pltpu.make_async_copy(grads.at[rows], grads_v.at[step], grads_sem.at[step]),
        ]
        for load in loads[step]:
            load.start()

    barrier = pltpu.get_barrier_semaphore()
    for shift in range(1, feat):
        pl.semaphore_signal(barrier, inc=1, device_id={"feat": lax.rem(me + shift, feat)}, device_id_type=MESH)
    for shift in range(1, stores):
        pl.semaphore_signal(barrier, inc=1, device_id={"store": lax.rem(core + shift, stores)}, device_id_type=MESH)

    row = lax.broadcasted_iota(jnp.int32, (rank, LANES), 0)
    lane = lax.broadcasted_iota(jnp.int32, (rank, LANES), 1)
    grad_place = (lane == (row % 2) * (rank // 2) + row // 2).astype(jnp.bfloat16)
    in_place = (lane == row + rank).astype(jnp.bfloat16)
    for load in basis_loads:
        load.wait()
    over_rank = (((0,), (0,)), ((), ()))
    in_wide = lax.dot_general(in_basis_v[...], in_place, over_rank, preferred_element_type=jnp.float32)
    grad_wide = lax.dot_general(grad_basis_v[...], grad_place, over_rank, preferred_element_type=jnp.float32)
    in_wide, grad_wide = in_wide.astype(jnp.bfloat16), grad_wide.astype(jnp.bfloat16)

    def project(step, half):
        rows = pl.ds(pl.multiple_of(half * block, block), block)
        return jnp.dot(acts_v[step, rows, :], in_wide, preferred_element_type=jnp.float32) + jnp.dot(
            grads_v[step, rows, :], grad_wide, preferred_element_type=jnp.float32
        )

    pair_copies = {}
    for index, step in enumerate(order):
        for load in loads[step]:
            load.wait()
        encode(pair_out.at[step], project(step, other))
        if index == 0:
            pl.semaphore_wait(barrier, feat - 1 + stores - 1)
        pair_copies[step] = remote(
            pair_out.at[step], pair_in.at[step], pair_send.at[step], pair_recv.at[step], {"feat": twin}
        )
        pair_copies[step].start()

    half = stored.shape[1] // HALVES
    stored_loads = []
    for part in range(HALVES):
        columns = pl.ds(part * half, half)
        load = pltpu.make_async_copy(stored.at[:, columns], stored_v.at[part], stored_sem.at[part])
        load.start()
        stored_loads.append(load)

    for step in order:
        partial[step] = project(step, my_pair)
    line_copies = {}
    total = None
    for step in order:
        pair_copies[step].wait_recv()
        both = partial[step] + decode(pair_in.at[step], block)
        if step == 0:
            total = both
        else:
            encode(line_out.at[step], both)
            spot = lax.rem(my_line + step, line)
            line_copies[step] = remote(
                line_out.at[step], line_in.at[step], line_send.at[step], line_recv.at[step],
                {"feat": spot * PAIR + my_pair},
            )
            line_copies[step].start()
    for step in order[:-1]:
        line_copies[step].wait_recv()
        total = total + decode(line_in.at[step], block)

    position = lax.broadcasted_iota(jnp.int32, (slots_per_doc, rank), 0)
    left = lax.broadcasted_iota(jnp.int32, (slots_per_doc, LANES), 1) < rank
    for doc in range(docs):
        length = lengths[me * docs + doc]
        rows = total[doc * slots_per_doc:(doc + 1) * slots_per_doc]
        grad_side = jnp.where(position < length, rows[:, :rank], 0.0)
        in_side = jnp.where(left, pltpu.roll(rows, rank, 1), rows)
        outer = lax.dot_general(
            grad_side, in_side, (((0,), (0,)), ((), ())),
            precision=lax.Precision.HIGHEST, preferred_element_type=jnp.float32,
        )
        query = jnp.where(left[:pairs], outer[:pairs], outer[pairs:]) / length.astype(jnp.float32)
        query = query.astype(jnp.bfloat16)
        for part in range(HALVES):
            gathered[part, core, me, pl.ds(doc * part_rows, part_rows), :] = query[part * part_rows:(part + 1) * part_rows]

    sent = []
    for part in range(HALVES):
        own = gathered.at[part, core, me]
        for shift in range(1, feat):
            sent.append(remote(
                own, own, all_send.at[part, shift], all_recv.at[part, shift], {"feat": lax.rem(me + shift, feat)}
            ))
            sent[-1].start()
    for part in range(HALVES):
        for shift in range(1, feat):
            there = gathered.at[part, core, lax.rem(me + feat - shift, feat)]
            remote(
                there, there, all_send.at[part, shift], all_recv.at[part, shift], {"feat": lax.rem(me + shift, feat)}
            ).wait_recv()
        blocks = gathered.at[part, core]
        for hop in range(1, stores):
            sent.append(remote(
                blocks, blocks, core_send.at[part, hop], core_recv.at[part, hop],
                {"store": lax.rem(core + hop, stores)},
            ))
            sent[-1].start()

    wide_rows = wide.shape[0]
    all_docs = scores.shape[0]
    queries[...] = jnp.zeros_like(queries)
    tile = 256
    for part in range(HALVES):
        for hop in range(1, stores):
            blocks = gathered.at[part, lax.rem(core + stores - hop, stores)]
            remote(
                blocks, blocks, core_send.at[part, hop], core_recv.at[part, hop],
                {"store": lax.rem(core + hop, stores)},
            ).wait_recv()
        wide[...] = gathered[part].reshape(wide_rows, LANES).astype(jnp.float32)
        for pair in range(part_rows):
            queries[:all_docs, pair * LANES:(pair + 1) * LANES] = wide[pl.ds(pair, all_docs, part_rows), :].astype(
                jnp.bfloat16
            )
        stored_loads[part].wait()
        for start in range(0, stored.shape[0], tile):
            product = lax.dot_general(
                stored_v[part, start:start + tile, :], queries[...], (((1,), (1,)), ((), ())),
                preferred_element_type=jnp.float32,
            )
            if part:
                product = product + sums[start:start + tile]
            if part + 1 < HALVES:
                sums[start:start + tile] = product
            else:
                scores[:, start:start + tile] = product.T[:all_docs]

    for step in order:
        pair_copies[step].wait_send()
        if step:
            line_copies[step].wait_send()
    for copy in sent:
        copy.wait_send()


def per_device(feat, stores, activations, output_grads, input_basis, grad_basis, lengths, stored_grads):
    tokens, features = activations.shape
    slots_per_doc = tokens // lengths.shape[0]
    rank = input_basis.shape[1]
    rows, depth = stored_grads.shape
    docs = lengths.shape[0] * stores
    padded = -(-docs // LANES) * LANES
    line = feat // PAIR
    block = tokens // feat
    part_rows = rank * rank // LANES // HALVES
    share = block // slots_per_doc * part_rows
    bf16, f32 = jnp.bfloat16, jnp.float32
    dma = pltpu.SemaphoreType.DMA
    anywhere = pl.BlockSpec(memory_space=pl.ANY)
    return pl.pallas_call(
        functools.partial(kernel, feat, stores, slots_per_doc),
        out_shape=jax.ShapeDtypeStruct((docs, rows), f32),
        in_specs=[anywhere] * 4 + [pl.BlockSpec(memory_space=pltpu.SMEM), anywhere],
        out_specs=pl.BlockSpec(memory_space=pltpu.VMEM),
        scratch_shapes=[
            pltpu.VMEM((line, PAIR * block, features), bf16),
            pltpu.VMEM((line, PAIR * block, features), bf16),
            pltpu.VMEM((rank, features), bf16),
            pltpu.VMEM((rank, features), bf16),
            pltpu.VMEM((HALVES, rows, depth // HALVES), bf16),
            pltpu.VMEM((line, block, LANES), f32),
            pltpu.VMEM((line, block + HEADER, LANES), jnp.int16),
            pltpu.VMEM((line, block + HEADER, LANES), jnp.int16),
            pltpu.VMEM((line, block + HEADER, LANES), jnp.int16),
            pltpu.VMEM((line, block + HEADER, LANES), jnp.int16),
            pltpu.VMEM((HALVES, stores, feat, share, LANES), bf16),
            pltpu.VMEM((docs * part_rows, LANES), f32),
            pltpu.VMEM((padded, depth // HALVES), bf16),
            pltpu.VMEM((rows, padded), f32),
            dma((line,)), dma((line,)), dma((2,)), dma((HALVES,)),
            dma((line,)), dma((line,)), dma((line,)), dma((line,)),
            dma((HALVES, feat)), dma((HALVES, feat)),
            dma((HALVES, stores)), dma((HALVES, stores)),
        ],
        compiler_params=pltpu.CompilerParams(
            collective_id=0, has_side_effects=True, vmem_limit_bytes=56 * 1024 * 1024
        ),
        cost_estimate=pl.CostEstimate(
            flops=4 * tokens * features * rank + 2 * docs * rows * depth,
            bytes_accessed=4 * tokens * features + 2 * rows * depth + 4 * docs * rows,
            transcendentals=0,
        ),
    )(activations, output_grads, input_basis.T, grad_basis.T, lengths, stored_grads)


def solution(mesh):
    placed = (
        P(("groups", "store"), "feat"),
        P(("groups", "store"), "feat"),
        P("feat", None),
        P("feat", None),
        P(("groups", "store")),
        P(("groups", "feat", "store"), None),
    )
    return jax.shard_map(
        functools.partial(per_device, mesh.shape["feat"], mesh.shape["store"]),
        mesh=mesh,
        in_specs=placed,
        out_specs=P("groups", ("feat", "store")),
        check_vma=False,
    )
```

```python
import functools

import jax
import jax.numpy as jnp
from jax import lax
from jax.experimental import pallas as pl
from jax.experimental.pallas import tpu as pltpu
from jax.sharding import PartitionSpec as P

MESH = pl.DeviceIdType.MESH
PAIR = 2
HALVES = 2
LANES = 128
HEADER = 16


def remote(src, dst, send_sem, recv_sem, target):
    return pltpu.make_async_remote_copy(
        src_ref=src, dst_ref=dst, send_sem=send_sem, recv_sem=recv_sem, device_id=target, device_id_type=MESH
    )


def encode(ref, values):
    block = values.shape[0]
    top = jnp.max(jnp.abs(values), axis=0, keepdims=True)
    power = 14.0 - jnp.floor(jnp.log2(jnp.maximum(top, 1e-30)))
    scaled = jnp.clip(jnp.round(values * jnp.exp2(power)), -32767.0, 32767.0)
    ref[:block] = scaled.astype(jnp.int32).astype(jnp.int16)
    ref[block:] = jnp.broadcast_to(power, (ref.shape[0] - block, LANES)).astype(jnp.int32).astype(jnp.int16)


def decode(ref, block):
    values = ref[:block].astype(jnp.int32).astype(jnp.float32)
    power = ref[block:].astype(jnp.int32).astype(jnp.float32)[:1]
    return values * jnp.exp2(-power)


def kernel(
    feat, stores, slots_per_doc,
    acts, grads, in_basis, grad_basis, lengths, stored, scores,
    acts_v, grads_v, in_basis_v, grad_basis_v, stored_v, partial,
    pair_out, pair_in, line_out, line_in, gathered, wide, queries, sums,
    acts_sem, grads_sem, basis_sem, stored_sem,
    pair_send, pair_recv, line_send, line_recv, all_send, all_recv, core_send, core_recv,
):
    line = feat // PAIR
    block = acts_v.shape[2]
    docs = block // slots_per_doc
    rank = in_basis.shape[0]
    pairs = rank * rank // LANES
    part_rows = pairs // HALVES
    order = list(range(1, line)) + [0]

    me = lax.axis_index("feat")
    core = lax.axis_index("store")
    my_line, my_pair = me // PAIR, lax.rem(me, PAIR)
    other = 1 - my_pair
    twin = my_line * PAIR + other

    barrier = pltpu.get_barrier_semaphore()
    for shift in range(1, feat):
        pl.semaphore_signal(barrier, inc=1, device_id={"feat": lax.rem(me + shift, feat)}, device_id_type=MESH)
    for shift in range(1, stores):
        pl.semaphore_signal(barrier, inc=1, device_id={"store": lax.rem(core + shift, stores)}, device_id_type=MESH)

    basis_loads = [
        pltpu.make_async_copy(in_basis, in_basis_v, basis_sem.at[0]),
        pltpu.make_async_copy(grad_basis, grad_basis_v, basis_sem.at[1]),
    ]
    for load in basis_loads:
        load.start()
    loads = {}
    for side, half in enumerate((other, my_pair)):
        for step in order:
            spot = lax.rem(my_line + step, line)
            rows = pl.ds(pl.multiple_of((spot * PAIR + half) * block, block), block)
            loads[side, step] = [
                pltpu.make_async_copy(acts.at[rows], acts_v.at[side, step], acts_sem.at[side, step]),
                pltpu.make_async_copy(grads.at[rows], grads_v.at[side, step], grads_sem.at[side, step]),
            ]
            for load in loads[side, step]:
                load.start()

    row = lax.broadcasted_iota(jnp.int32, (rank, LANES), 0)
    lane = lax.broadcasted_iota(jnp.int32, (rank, LANES), 1)
    grad_place = (lane == (row % 2) * (rank // 2) + row // 2).astype(jnp.bfloat16)
    in_place = (lane == row + rank).astype(jnp.bfloat16)
    for load in basis_loads:
        load.wait()
    over_rank = (((0,), (0,)), ((), ()))
    in_wide = lax.dot_general(in_basis_v[...], in_place, over_rank, preferred_element_type=jnp.float32)
    grad_wide = lax.dot_general(grad_basis_v[...], grad_place, over_rank, preferred_element_type=jnp.float32)
    in_wide, grad_wide = in_wide.astype(jnp.bfloat16), grad_wide.astype(jnp.bfloat16)

    def project(side, step):
        for load in loads[side, step]:
            load.wait()
        return jnp.dot(acts_v[side, step], in_wide, preferred_element_type=jnp.float32) + jnp.dot(
            grads_v[side, step], grad_wide, preferred_element_type=jnp.float32
        )

    pair_copies = {}
    for index, step in enumerate(order):
        encode(pair_out.at[step], project(0, step))
        if index == 0:
            pl.semaphore_wait(barrier, feat - 1 + stores - 1)
        pair_copies[step] = remote(
            pair_out.at[step], pair_in.at[step], pair_send.at[step], pair_recv.at[step], {"feat": twin}
        )
        pair_copies[step].start()

    queries[...] = jnp.zeros_like(queries)
    half = stored.shape[1] // HALVES
    stored_loads = []
    for part in range(HALVES):
        columns = pl.ds(part * half, half)
        load = pltpu.make_async_copy(stored.at[:, columns], stored_v.at[part], stored_sem.at[part])
        load.start()
        stored_loads.append(load)

    for step in order:
        partial[step] = project(1, step)
    line_copies = {}
    total = None
    for step in order:
        pair_copies[step].wait_recv()
        both = partial[step] + decode(pair_in.at[step], block)
        if step == 0:
            total = both
        else:
            encode(line_out.at[step], both)
            spot = lax.rem(my_line + step, line)
            line_copies[step] = remote(
                line_out.at[step], line_in.at[step], line_send.at[step], line_recv.at[step],
                {"feat": spot * PAIR + my_pair},
            )
            line_copies[step].start()
    for step in order[:-1]:
        line_copies[step].wait_recv()
        total = total + decode(line_in.at[step], block)

    position = lax.broadcasted_iota(jnp.int32, (slots_per_doc, rank), 0)
    left = lax.broadcasted_iota(jnp.int32, (slots_per_doc, LANES), 1) < rank
    for doc in range(docs):
        length = lengths[me * docs + doc]
        rows = total[doc * slots_per_doc:(doc + 1) * slots_per_doc]
        grad_side = jnp.where(position < length, rows[:, :rank], 0.0)
        in_side = jnp.where(left, pltpu.roll(rows, rank, 1), rows)
        grad_high, in_high = grad_side.astype(jnp.bfloat16), in_side.astype(jnp.bfloat16)
        grad_low = (grad_side - grad_high.astype(jnp.float32)).astype(jnp.bfloat16)
        in_low = (in_side - in_high.astype(jnp.float32)).astype(jnp.bfloat16)
        outer = lax.dot_general(
            jnp.concatenate([grad_high, grad_high, grad_low]), jnp.concatenate([in_high, in_low, in_high]),
            (((0,), (0,)), ((), ())), preferred_element_type=jnp.float32,
        )
        query = jnp.where(left[:pairs], outer[:pairs], outer[pairs:]) / length.astype(jnp.float32)
        query = query.astype(jnp.bfloat16)
        for part in range(HALVES):
            gathered[part, core, me, pl.ds(doc * part_rows, part_rows), :] = query[part * part_rows:(part + 1) * part_rows]

    sent = []
    for part in range(HALVES):
        own = gathered.at[part, core, me]
        for shift in range(1, feat):
            sent.append(remote(
                own, own, all_send.at[part, shift], all_recv.at[part, shift], {"feat": lax.rem(me + shift, feat)}
            ))
            sent[-1].start()
    for part in range(HALVES):
        for shift in range(1, feat):
            there = gathered.at[part, core, lax.rem(me + feat - shift, feat)]
            remote(
                there, there, all_send.at[part, shift], all_recv.at[part, shift], {"feat": lax.rem(me + shift, feat)}
            ).wait_recv()
        blocks = gathered.at[part, core]
        for hop in range(1, stores):
            sent.append(remote(
                blocks, blocks, core_send.at[part, hop], core_recv.at[part, hop],
                {"store": lax.rem(core + hop, stores)},
            ))
            sent[-1].start()

    core_docs = scores.shape[0] // stores
    span = queries.shape[1] // stores

    def lay_out(part, source, place):
        wide[...] = gathered[part, source].reshape(wide.shape).astype(jnp.float32)
        for pair in range(part_rows):
            queries[part, place * span:place * span + core_docs, pair * LANES:(pair + 1) * LANES] = wide[
                pl.ds(pair, core_docs, part_rows), :
            ].astype(jnp.bfloat16)

    for part in range(HALVES):
        lay_out(part, core, 0)
    tile = 256
    for part in range(HALVES):
        for hop in range(1, stores):
            source = lax.rem(core + stores - hop, stores)
            blocks = gathered.at[part, source]
            remote(
                blocks, blocks, core_send.at[part, hop], core_recv.at[part, hop],
                {"store": lax.rem(core + hop, stores)},
            ).wait_recv()
            lay_out(part, source, hop)
        stored_loads[part].wait()
        for start in range(0, stored.shape[0], tile):
            product = lax.dot_general(
                stored_v[part, start:start + tile, :], queries[part], (((1,), (1,)), ((), ())),
                preferred_element_type=jnp.float32,
            )
            if part:
                product = product + sums[start:start + tile]
            if part + 1 < HALVES:
                sums[start:start + tile] = product
                continue
            turned = product.T
            for hop in range(stores):
                rows = pl.ds(pl.multiple_of(lax.rem(core + stores - hop, stores) * core_docs, core_docs), core_docs)
                scores[rows, start:start + tile] = turned[hop * span:hop * span + core_docs]

    for step in order:
        pair_copies[step].wait_send()
        if step:
            line_copies[step].wait_send()
    for copy in sent:
        copy.wait_send()


def per_device(feat, stores, activations, output_grads, input_basis, grad_basis, lengths, stored_grads):
    tokens, features = activations.shape
    slots_per_doc = tokens // lengths.shape[0]
    rank = input_basis.shape[1]
    rows, depth = stored_grads.shape
    docs = lengths.shape[0] * stores
    padded = -(-docs // LANES) * LANES
    line = feat // PAIR
    block = tokens // feat
    part_rows = rank * rank // LANES // HALVES
    share = block // slots_per_doc * part_rows
    bf16, f32 = jnp.bfloat16, jnp.float32
    dma = pltpu.SemaphoreType.DMA
    anywhere = pl.BlockSpec(memory_space=pl.ANY)
    return pl.pallas_call(
        functools.partial(kernel, feat, stores, slots_per_doc),
        out_shape=jax.ShapeDtypeStruct((docs, rows), f32),
        in_specs=[anywhere] * 4 + [pl.BlockSpec(memory_space=pltpu.SMEM), anywhere],
        out_specs=pl.BlockSpec(memory_space=pltpu.VMEM),
        scratch_shapes=[
            pltpu.VMEM((2, line, block, features), bf16),
            pltpu.VMEM((2, line, block, features), bf16),
            pltpu.VMEM((rank, features), bf16),
            pltpu.VMEM((rank, features), bf16),
            pltpu.VMEM((HALVES, rows, depth // HALVES), bf16),
            pltpu.VMEM((line, block, LANES), f32),
            pltpu.VMEM((line, block + HEADER, LANES), jnp.int16),
            pltpu.VMEM((line, block + HEADER, LANES), jnp.int16),
            pltpu.VMEM((line, block + HEADER, LANES), jnp.int16),
            pltpu.VMEM((line, block + HEADER, LANES), jnp.int16),
            pltpu.VMEM((HALVES, stores, feat, share, LANES), bf16),
            pltpu.VMEM((docs // stores * part_rows, LANES), f32),
            pltpu.VMEM((HALVES, padded, depth // HALVES), bf16),
            pltpu.VMEM((rows, padded), f32),
            dma((2, line)), dma((2, line)), dma((2,)), dma((HALVES,)),
            dma((line,)), dma((line,)), dma((line,)), dma((line,)),
            dma((HALVES, feat)), dma((HALVES, feat)),
            dma((HALVES, stores)), dma((HALVES, stores)),
        ],
        compiler_params=pltpu.CompilerParams(
            collective_id=0, has_side_effects=True, vmem_limit_bytes=53 * 1024 * 1024
        ),
        cost_estimate=pl.CostEstimate(
            flops=4 * tokens * features * rank + 2 * docs * rows * depth,
            bytes_accessed=4 * tokens * features + 2 * rows * depth + 4 * docs * rows,
            transcendentals=0,
        ),
    )(activations, output_grads, input_basis.T, grad_basis.T, lengths, stored_grads)


def solution(mesh):
    placed = (
        P(("groups", "store"), "feat"),
        P(("groups", "store"), "feat"),
        P("feat", None),
        P("feat", None),
        P(("groups", "store")),
        P(("groups", "feat", "store"), None),
    )
    return jax.shard_map(
        functools.partial(per_device, mesh.shape["feat"], mesh.shape["store"]),
        mesh=mesh,
        in_specs=placed,
        out_specs=P("groups", ("feat", "store")),
        check_vma=False,
    )
```

```python
import functools

import jax
import jax.numpy as jnp
from jax import lax
from jax.experimental import pallas as pl
from jax.experimental.pallas import tpu as pltpu
from jax.sharding import PartitionSpec as P

MESH = pl.DeviceIdType.MESH
PAIR = 2
HALVES = 2
LANES = 128
HEADER = 16


def remote(src, dst, send_sem, recv_sem, target):
    return pltpu.make_async_remote_copy(
        src_ref=src, dst_ref=dst, send_sem=send_sem, recv_sem=recv_sem, device_id=target, device_id_type=MESH
    )


def encode(ref, values):
    block = values.shape[0]
    top = jnp.max(jnp.abs(values), axis=0, keepdims=True)
    power = 14.0 - jnp.floor(jnp.log2(jnp.maximum(top, 1e-30)))
    scaled = jnp.clip(jnp.round(values * jnp.exp2(power)), -32767.0, 32767.0)
    ref[:block] = scaled.astype(jnp.int32).astype(jnp.int16)
    ref[block:] = jnp.broadcast_to(power, (ref.shape[0] - block, LANES)).astype(jnp.int32).astype(jnp.int16)


def decode(ref, block):
    values = ref[:block].astype(jnp.int32).astype(jnp.float32)
    power = ref[block:].astype(jnp.int32).astype(jnp.float32)[:1]
    return values * jnp.exp2(-power)


def kernel(
    feat, stores, slots_per_doc,
    acts, grads, in_basis, grad_basis, lengths, stored, scores,
    acts_v, grads_v, in_basis_v, grad_basis_v, lengths_s, stored_v, partial,
    pair_out, pair_in, line_out, line_in, gathered, wide, queries, sums,
    acts_sem, grads_sem, basis_sem, lengths_sem, stored_sem,
    pair_send, pair_recv, line_send, line_recv, all_send, all_recv, core_send, core_recv,
):
    line = feat // PAIR
    block = acts_v.shape[2]
    docs = block // slots_per_doc
    rank = in_basis.shape[0]
    pairs = rank * rank // LANES
    part_rows = pairs // HALVES
    order = list(range(1, line)) + [0]

    me = lax.axis_index("feat")
    core = lax.axis_index("store")
    my_line, my_pair = me // PAIR, lax.rem(me, PAIR)
    other = 1 - my_pair
    twin = my_line * PAIR + other

    barrier = pltpu.get_barrier_semaphore()
    for shift in range(1, feat):
        pl.semaphore_signal(barrier, inc=1, device_id={"feat": lax.rem(me + shift, feat)}, device_id_type=MESH)
    for shift in range(1, stores):
        pl.semaphore_signal(barrier, inc=1, device_id={"store": lax.rem(core + shift, stores)}, device_id_type=MESH)

    basis_loads = [
        pltpu.make_async_copy(in_basis, in_basis_v, basis_sem.at[0]),
        pltpu.make_async_copy(grad_basis, grad_basis_v, basis_sem.at[1]),
    ]
    for load in basis_loads:
        load.start()
    loads = {}
    for side, half in enumerate((other, my_pair)):
        for step in order:
            spot = lax.rem(my_line + step, line)
            rows = pl.ds(pl.multiple_of((spot * PAIR + half) * block, block), block)
            loads[side, step] = [
                pltpu.make_async_copy(acts.at[rows], acts_v.at[side, step], acts_sem.at[side, step]),
                pltpu.make_async_copy(grads.at[rows], grads_v.at[side, step], grads_sem.at[side, step]),
            ]
            for load in loads[side, step]:
                load.start()

    row = lax.broadcasted_iota(jnp.int32, (rank, LANES), 0)
    lane = lax.broadcasted_iota(jnp.int32, (rank, LANES), 1)
    grad_place = (lane == (row % 2) * (rank // 2) + row // 2).astype(jnp.bfloat16)
    in_place = (lane == row + rank).astype(jnp.bfloat16)
    for load in basis_loads:
        load.wait()
    over_rank = (((0,), (0,)), ((), ()))
    in_wide = lax.dot_general(in_basis_v[...], in_place, over_rank, preferred_element_type=jnp.float32)
    grad_wide = lax.dot_general(grad_basis_v[...], grad_place, over_rank, preferred_element_type=jnp.float32)
    in_wide, grad_wide = in_wide.astype(jnp.bfloat16), grad_wide.astype(jnp.bfloat16)

    def project(side, step):
        for load in loads[side, step]:
            load.wait()
        return jnp.dot(acts_v[side, step], in_wide, preferred_element_type=jnp.float32) + jnp.dot(
            grads_v[side, step], grad_wide, preferred_element_type=jnp.float32
        )

    pair_copies = {}
    for index, step in enumerate(order):
        encode(pair_out.at[step], project(0, step))
        if index == 0:
            pl.semaphore_wait(barrier, feat - 1 + stores - 1)
        pair_copies[step] = remote(
            pair_out.at[step], pair_in.at[step], pair_send.at[step], pair_recv.at[step], {"feat": twin}
        )
        pair_copies[step].start()

    queries[...] = jnp.zeros_like(queries)
    lengths_load = pltpu.make_async_copy(lengths, lengths_s, lengths_sem)
    lengths_load.start()
    half = stored.shape[1] // HALVES
    stored_loads = []
    for part in range(HALVES):
        columns = pl.ds(part * half, half)
        load = pltpu.make_async_copy(stored.at[:, columns], stored_v.at[part], stored_sem.at[part])
        load.start()
        stored_loads.append(load)

    for step in order:
        partial[step] = project(1, step)
    line_copies = {}
    total = None
    for step in order:
        pair_copies[step].wait_recv()
        both = partial[step] + decode(pair_in.at[step], block)
        if step == 0:
            total = both
        else:
            encode(line_out.at[step], both)
            spot = lax.rem(my_line + step, line)
            line_copies[step] = remote(
                line_out.at[step], line_in.at[step], line_send.at[step], line_recv.at[step],
                {"feat": spot * PAIR + my_pair},
            )
            line_copies[step].start()
    for step in order[:-1]:
        line_copies[step].wait_recv()
        total = total + decode(line_in.at[step], block)

    lengths_load.wait()
    position = lax.broadcasted_iota(jnp.int32, (slots_per_doc, rank), 0)
    left = lax.broadcasted_iota(jnp.int32, (slots_per_doc, LANES), 1) < rank
    for doc in range(docs):
        length = lengths_s[me * docs + doc]
        rows = total[doc * slots_per_doc:(doc + 1) * slots_per_doc]
        grad_side = jnp.where(position < length, rows[:, :rank], 0.0)
        in_side = jnp.where(left, pltpu.roll(rows, rank, 1), rows)
        grad_high, in_high = grad_side.astype(jnp.bfloat16), in_side.astype(jnp.bfloat16)
        grad_low = (grad_side - grad_high.astype(jnp.float32)).astype(jnp.bfloat16)
        in_low = (in_side - in_high.astype(jnp.float32)).astype(jnp.bfloat16)
        outer = lax.dot_general(
            jnp.concatenate([grad_high, grad_high, grad_low]), jnp.concatenate([in_high, in_low, in_high]),
            (((0,), (0,)), ((), ())), preferred_element_type=jnp.float32,
        )
        query = jnp.where(left[:pairs], outer[:pairs], outer[pairs:]) / length.astype(jnp.float32)
        query = query.astype(jnp.bfloat16)
        for part in range(HALVES):
            gathered[part, core, me, pl.ds(doc * part_rows, part_rows), :] = query[part * part_rows:(part + 1) * part_rows]

    sent = []
    for part in range(HALVES):
        own = gathered.at[part, core, me]
        for shift in range(1, feat):
            sent.append(remote(
                own, own, all_send.at[part, shift], all_recv.at[part, shift], {"feat": lax.rem(me + shift, feat)}
            ))
            sent[-1].start()
    for part in range(HALVES):
        for shift in range(1, feat):
            there = gathered.at[part, core, lax.rem(me + feat - shift, feat)]
            remote(
                there, there, all_send.at[part, shift], all_recv.at[part, shift], {"feat": lax.rem(me + shift, feat)}
            ).wait_recv()
        blocks = gathered.at[part, core]
        for hop in range(1, stores):
            sent.append(remote(
                blocks, blocks, core_send.at[part, hop], core_recv.at[part, hop],
                {"store": lax.rem(core + hop, stores)},
            ))
            sent[-1].start()

    core_docs = scores.shape[0] // stores
    span = queries.shape[1] // stores

    def lay_out(part, source, place):
        wide[...] = gathered[part, source].reshape(wide.shape).astype(jnp.float32)
        for pair in range(part_rows):
            queries[part, place * span:place * span + core_docs, pair * LANES:(pair + 1) * LANES] = wide[
                pl.ds(pair, core_docs, part_rows), :
            ].astype(jnp.bfloat16)

    for part in range(HALVES):
        lay_out(part, core, 0)
    tile = 256
    for part in range(HALVES):
        for hop in range(1, stores):
            source = lax.rem(core + stores - hop, stores)
            blocks = gathered.at[part, source]
            remote(
                blocks, blocks, core_send.at[part, hop], core_recv.at[part, hop],
                {"store": lax.rem(core + hop, stores)},
            ).wait_recv()
            lay_out(part, source, hop)
        stored_loads[part].wait()
        for start in range(0, stored.shape[0], tile):
            product = lax.dot_general(
                stored_v[part, start:start + tile, :], queries[part], (((1,), (1,)), ((), ())),
                preferred_element_type=jnp.float32,
            )
            if part:
                product = product + sums[start:start + tile]
            if part + 1 < HALVES:
                sums[start:start + tile] = product
                continue
            turned = product.T
            for hop in range(stores):
                rows = pl.ds(pl.multiple_of(lax.rem(core + stores - hop, stores) * core_docs, core_docs), core_docs)
                scores[rows, start:start + tile] = turned[hop * span:hop * span + core_docs]

    for step in order:
        pair_copies[step].wait_send()
        if step:
            line_copies[step].wait_send()
    for copy in sent:
        copy.wait_send()


def per_device(feat, stores, activations, output_grads, input_basis, grad_basis, lengths, stored_grads):
    tokens, features = activations.shape
    slots_per_doc = tokens // lengths.shape[0]
    rank = input_basis.shape[1]
    rows, depth = stored_grads.shape
    docs = lengths.shape[0] * stores
    padded = -(-docs // LANES) * LANES
    line = feat // PAIR
    block = tokens // feat
    part_rows = rank * rank // LANES // HALVES
    share = block // slots_per_doc * part_rows
    bf16, f32 = jnp.bfloat16, jnp.float32
    dma = pltpu.SemaphoreType.DMA
    anywhere = pl.BlockSpec(memory_space=pl.ANY)
    return pl.pallas_call(
        functools.partial(kernel, feat, stores, slots_per_doc),
        out_shape=pltpu.VMEM((docs, rows), f32),
        in_specs=[anywhere] * 6,
        out_specs=pl.BlockSpec(memory_space=pltpu.VMEM),
        scratch_shapes=[
            pltpu.VMEM((2, line, block, features), bf16),
            pltpu.VMEM((2, line, block, features), bf16),
            pltpu.VMEM((rank, features), bf16),
            pltpu.VMEM((rank, features), bf16),
            pltpu.SMEM(lengths.shape, jnp.int32),
            pltpu.VMEM((HALVES, rows, depth // HALVES), bf16),
            pltpu.VMEM((line, block, LANES), f32),
            pltpu.VMEM((line, block + HEADER, LANES), jnp.int16),
            pltpu.VMEM((line, block + HEADER, LANES), jnp.int16),
            pltpu.VMEM((line, block + HEADER, LANES), jnp.int16),
            pltpu.VMEM((line, block + HEADER, LANES), jnp.int16),
            pltpu.VMEM((HALVES, stores, feat, share, LANES), bf16),
            pltpu.VMEM((docs // stores * part_rows, LANES), f32),
            pltpu.VMEM((HALVES, padded, depth // HALVES), bf16),
            pltpu.VMEM((rows, padded), f32),
            dma((2, line)), dma((2, line)), dma((2,)), dma(()), dma((HALVES,)),
            dma((line,)), dma((line,)), dma((line,)), dma((line,)),
            dma((HALVES, feat)), dma((HALVES, feat)),
            dma((HALVES, stores)), dma((HALVES, stores)),
        ],
        compiler_params=pltpu.CompilerParams(
            collective_id=0, has_side_effects=True, vmem_limit_bytes=53 * 1024 * 1024
        ),
        cost_estimate=pl.CostEstimate(
            flops=4 * tokens * features * rank + 2 * docs * rows * depth,
            bytes_accessed=4 * tokens * features + 2 * rows * depth + 4 * docs * rows,
            transcendentals=0,
        ),
    )(*[
        pltpu.with_memory_space_constraint(operand, pltpu.HBM)
        for operand in (activations, output_grads, input_basis.T, grad_basis.T, lengths, stored_grads)
    ])


def solution(mesh):
    placed = (
        P(("groups", "store"), "feat"),
        P(("groups", "store"), "feat"),
        P("feat", None),
        P("feat", None),
        P(("groups", "store")),
        P(("groups", "feat", "store"), None),
    )
    return jax.shard_map(
        functools.partial(per_device, mesh.shape["feat"], mesh.shape["store"]),
        mesh=mesh,
        in_specs=placed,
        out_specs=P("groups", ("feat", "store")),
        check_vma=False,
    )
```

```python
import functools

import jax
import jax.numpy as jnp
from jax import lax
from jax.experimental import pallas as pl
from jax.experimental.pallas import tpu as pltpu
from jax.sharding import PartitionSpec as P

MESH = pl.DeviceIdType.MESH
PAIR = 2
HALVES = 2
LANES = 128
AHEAD = 3
HEADER = 16


def remote(src, dst, send_sem, recv_sem, target):
    return pltpu.make_async_remote_copy(
        src_ref=src, dst_ref=dst, send_sem=send_sem, recv_sem=recv_sem, device_id=target, device_id_type=MESH
    )


def encode(ref, values):
    block = values.shape[0]
    top = jnp.max(jnp.abs(values), axis=0, keepdims=True)
    power = 14.0 - jnp.floor(jnp.log2(jnp.maximum(top, 1e-30)))
    scaled = jnp.clip(jnp.round(values * jnp.exp2(power)), -32767.0, 32767.0)
    ref[:block] = scaled.astype(jnp.int32).astype(jnp.int16)
    ref[block:] = jnp.broadcast_to(power, (ref.shape[0] - block, LANES)).astype(jnp.int32).astype(jnp.int16)


def decode(ref, block):
    values = ref[:block].astype(jnp.int32).astype(jnp.float32)
    power = ref[block:].astype(jnp.int32).astype(jnp.float32)[:1]
    return values * jnp.exp2(-power)


def kernel(
    feat, stores, slots_per_doc,
    acts, grads, in_basis, grad_basis, lengths, stored, scores,
    acts_v, grads_v, in_basis_v, grad_basis_v, lengths_s, stored_v,
    pair_out, pair_in, line_out, line_in, gathered, wide, queries, sums,
    acts_sem, grads_sem, basis_sem, lengths_sem, stored_sem,
    pair_send, pair_recv, line_send, line_recv, all_send, all_recv, core_send, core_recv,
):
    line = feat // PAIR
    block = acts_v.shape[2]
    docs = block // slots_per_doc
    rank = in_basis.shape[0]
    pairs = rank * rank // LANES
    part_rows = pairs // HALVES
    order = list(range(1, line)) + [0]

    me = lax.axis_index("feat")
    core = lax.axis_index("store")
    my_line, my_pair = me // PAIR, lax.rem(me, PAIR)
    other = 1 - my_pair
    twin = my_line * PAIR + other

    basis_loads = [
        pltpu.make_async_copy(in_basis, in_basis_v, basis_sem.at[0]),
        pltpu.make_async_copy(grad_basis, grad_basis_v, basis_sem.at[1]),
    ]
    for load in basis_loads:
        load.start()
    loads = {}
    for side, half in enumerate((other, my_pair)):
        for step in order:
            spot = lax.rem(my_line + step, line)
            rows = pl.ds(pl.multiple_of((spot * PAIR + half) * block, block), block)
            loads[side, step] = [
                pltpu.make_async_copy(acts.at[rows], acts_v.at[side, step], acts_sem.at[side, step]),
                pltpu.make_async_copy(grads.at[rows], grads_v.at[side, step], grads_sem.at[side, step]),
            ]
    waiting = list(loads.values())

    def start_next():
        if waiting:
            for load in waiting.pop(0):
                load.start()

    for _ in range(AHEAD):
        start_next()

    barrier = pltpu.get_barrier_semaphore()
    for shift in range(1, feat):
        pl.semaphore_signal(barrier, inc=1, device_id={"feat": lax.rem(me + shift, feat)}, device_id_type=MESH)
    for shift in range(1, stores):
        pl.semaphore_signal(barrier, inc=1, device_id={"store": lax.rem(core + shift, stores)}, device_id_type=MESH)

    row = lax.broadcasted_iota(jnp.int32, (rank, LANES), 0)
    lane = lax.broadcasted_iota(jnp.int32, (rank, LANES), 1)
    grad_place = (lane == (row % 2) * (rank // 2) + row // 2).astype(jnp.bfloat16)
    in_place = (lane == row + rank).astype(jnp.bfloat16)
    for load in basis_loads:
        load.wait()
    over_rank = (((0,), (0,)), ((), ()))
    in_wide = lax.dot_general(in_basis_v[...], in_place, over_rank, preferred_element_type=jnp.float32)
    grad_wide = lax.dot_general(grad_basis_v[...], grad_place, over_rank, preferred_element_type=jnp.float32)
    in_wide, grad_wide = in_wide.astype(jnp.bfloat16), grad_wide.astype(jnp.bfloat16)

    def project(side, step):
        for load in loads[side, step]:
            load.wait()
        start_next()
        return jnp.dot(acts_v[side, step], in_wide, preferred_element_type=jnp.float32) + jnp.dot(
            grads_v[side, step], grad_wide, preferred_element_type=jnp.float32
        )

    pair_copies = {}
    for index, step in enumerate(order):
        encode(pair_out.at[step], project(0, step))
        if index == 0:
            pl.semaphore_wait(barrier, feat - 1 + stores - 1)
        pair_copies[step] = remote(
            pair_out.at[step], pair_in.at[step], pair_send.at[step], pair_recv.at[step], {"feat": twin}
        )
        pair_copies[step].start()

    queries[...] = jnp.zeros_like(queries)
    lengths_load = pltpu.make_async_copy(lengths, lengths_s, lengths_sem)
    lengths_load.start()
    half = stored.shape[1] // HALVES
    stored_loads = []
    for part in range(HALVES):
        columns = pl.ds(part * half, half)
        load = pltpu.make_async_copy(stored.at[:, columns], stored_v.at[part], stored_sem.at[part])
        load.start()
        stored_loads.append(load)

    line_copies = {}
    total = None
    for step in order:
        own_half = project(1, step)
        pair_copies[step].wait_recv()
        both = own_half + decode(pair_in.at[step], block)
        if step == 0:
            total = both
        else:
            encode(line_out.at[step], both)
            spot = lax.rem(my_line + step, line)
            line_copies[step] = remote(
                line_out.at[step], line_in.at[step], line_send.at[step], line_recv.at[step],
                {"feat": spot * PAIR + my_pair},
            )
            line_copies[step].start()
    for step in order[:-1]:
        line_copies[step].wait_recv()
        total = total + decode(line_in.at[step], block)

    lengths_load.wait()
    position = lax.broadcasted_iota(jnp.int32, (slots_per_doc, rank), 0)
    left = lax.broadcasted_iota(jnp.int32, (slots_per_doc, LANES), 1) < rank
    for doc in range(docs):
        length = lengths_s[me * docs + doc]
        rows = total[doc * slots_per_doc:(doc + 1) * slots_per_doc]
        grad_side = jnp.where(position < length, rows[:, :rank], 0.0)
        in_side = jnp.where(left, pltpu.roll(rows, rank, 1), rows)
        grad_high, in_high = grad_side.astype(jnp.bfloat16), in_side.astype(jnp.bfloat16)
        grad_low = (grad_side - grad_high.astype(jnp.float32)).astype(jnp.bfloat16)
        in_low = (in_side - in_high.astype(jnp.float32)).astype(jnp.bfloat16)
        outer = lax.dot_general(
            jnp.concatenate([grad_high, grad_high, grad_low]), jnp.concatenate([in_high, in_low, in_high]),
            (((0,), (0,)), ((), ())), preferred_element_type=jnp.float32,
        )
        query = jnp.where(left[:pairs], outer[:pairs], outer[pairs:]) / length.astype(jnp.float32)
        query = query.astype(jnp.bfloat16)
        for part in range(HALVES):
            gathered[part, core, me, pl.ds(doc * part_rows, part_rows), :] = query[part * part_rows:(part + 1) * part_rows]

    sent = []
    for part in range(HALVES):
        own = gathered.at[part, core, me]
        for shift in range(1, feat):
            sent.append(remote(
                own, own, all_send.at[part, shift], all_recv.at[part, shift], {"feat": lax.rem(me + shift, feat)}
            ))
            sent[-1].start()
    for part in range(HALVES):
        for shift in range(1, feat):
            there = gathered.at[part, core, lax.rem(me + feat - shift, feat)]
            remote(
                there, there, all_send.at[part, shift], all_recv.at[part, shift], {"feat": lax.rem(me + shift, feat)}
            ).wait_recv()
        blocks = gathered.at[part, core]
        for hop in range(1, stores):
            sent.append(remote(
                blocks, blocks, core_send.at[part, hop], core_recv.at[part, hop],
                {"store": lax.rem(core + hop, stores)},
            ))
            sent[-1].start()

    core_docs = scores.shape[0] // stores
    span = queries.shape[1] // stores

    def lay_out(part, source, place):
        wide[...] = gathered[part, source].reshape(wide.shape).astype(jnp.float32)
        for pair in range(part_rows):
            queries[part, place * span:place * span + core_docs, pair * LANES:(pair + 1) * LANES] = wide[
                pl.ds(pair, core_docs, part_rows), :
            ].astype(jnp.bfloat16)

    for part in range(HALVES):
        lay_out(part, core, 0)
    tile = 256
    for part in range(HALVES):
        for hop in range(1, stores):
            source = lax.rem(core + stores - hop, stores)
            blocks = gathered.at[part, source]
            remote(
                blocks, blocks, core_send.at[part, hop], core_recv.at[part, hop],
                {"store": lax.rem(core + hop, stores)},
            ).wait_recv()
            lay_out(part, source, hop)
        stored_loads[part].wait()
        for start in range(0, stored.shape[0], tile):
            product = lax.dot_general(
                stored_v[part, start:start + tile, :], queries[part], (((1,), (1,)), ((), ())),
                preferred_element_type=jnp.float32,
            )
            if part:
                product = product + sums[start:start + tile]
            if part + 1 < HALVES:
                sums[start:start + tile] = product
                continue
            turned = product.T
            for hop in range(stores):
                rows = pl.ds(pl.multiple_of(lax.rem(core + stores - hop, stores) * core_docs, core_docs), core_docs)
                scores[rows, start:start + tile] = turned[hop * span:hop * span + core_docs]

    for step in order:
        pair_copies[step].wait_send()
        if step:
            line_copies[step].wait_send()
    for copy in sent:
        copy.wait_send()


def per_device(feat, stores, activations, output_grads, input_basis, grad_basis, lengths, stored_grads):
    tokens, features = activations.shape
    slots_per_doc = tokens // lengths.shape[0]
    rank = input_basis.shape[1]
    rows, depth = stored_grads.shape
    docs = lengths.shape[0] * stores
    padded = -(-docs // LANES) * LANES
    line = feat // PAIR
    block = tokens // feat
    part_rows = rank * rank // LANES // HALVES
    share = block // slots_per_doc * part_rows
    bf16, f32 = jnp.bfloat16, jnp.float32
    dma = pltpu.SemaphoreType.DMA
    anywhere = pl.BlockSpec(memory_space=pl.ANY)
    return pl.pallas_call(
        functools.partial(kernel, feat, stores, slots_per_doc),
        out_shape=pltpu.VMEM((docs, rows), f32),
        in_specs=[anywhere] * 6,
        out_specs=pl.BlockSpec(memory_space=pltpu.VMEM),
        scratch_shapes=[
            pltpu.VMEM((2, line, block, features), bf16),
            pltpu.VMEM((2, line, block, features), bf16),
            pltpu.VMEM((rank, features), bf16),
            pltpu.VMEM((rank, features), bf16),
            pltpu.SMEM(lengths.shape, jnp.int32),
            pltpu.VMEM((HALVES, rows, depth // HALVES), bf16),
            pltpu.VMEM((line, block + HEADER, LANES), jnp.int16),
            pltpu.VMEM((line, block + HEADER, LANES), jnp.int16),
            pltpu.VMEM((line, block + HEADER, LANES), jnp.int16),
            pltpu.VMEM((line, block + HEADER, LANES), jnp.int16),
            pltpu.VMEM((HALVES, stores, feat, share, LANES), bf16),
            pltpu.VMEM((docs // stores * part_rows, LANES), f32),
            pltpu.VMEM((HALVES, padded, depth // HALVES), bf16),
            pltpu.VMEM((rows, padded), f32),
            dma((2, line)), dma((2, line)), dma((2,)), dma(()), dma((HALVES,)),
            dma((line,)), dma((line,)), dma((line,)), dma((line,)),
            dma((HALVES, feat)), dma((HALVES, feat)),
            dma((HALVES, stores)), dma((HALVES, stores)),
        ],
        compiler_params=pltpu.CompilerParams(
            collective_id=0, has_side_effects=True, vmem_limit_bytes=53 * 1024 * 1024
        ),
        cost_estimate=pl.CostEstimate(
            flops=4 * tokens * features * rank + 2 * docs * rows * depth,
            bytes_accessed=4 * tokens * features + 2 * rows * depth + 4 * docs * rows,
            transcendentals=0,
        ),
    )(*[
        pltpu.with_memory_space_constraint(operand, pltpu.HBM)
        for operand in (activations, output_grads, input_basis.T, grad_basis.T, lengths, stored_grads)
    ])


def solution(mesh):
    placed = (
        P(("groups", "store"), "feat"),
        P(("groups", "store"), "feat"),
        P("feat", None),
        P("feat", None),
        P(("groups", "store")),
        P(("groups", "feat", "store"), None),
    )
    return jax.shard_map(
        functools.partial(per_device, mesh.shape["feat"], mesh.shape["store"]),
        mesh=mesh,
        in_specs=placed,
        out_specs=P("groups", ("feat", "store")),
        check_vma=False,
    )
```

```python
import functools

import jax
import jax.numpy as jnp
from jax import lax
from jax.experimental import pallas as pl
from jax.experimental.pallas import tpu as pltpu
from jax.sharding import PartitionSpec as P

MESH = pl.DeviceIdType.MESH
PAIR = 2
HALVES = 2
LANES = 128
AHEAD = 3
HEADER = 16


def remote(src, dst, send_sem, recv_sem, target):
    return pltpu.make_async_remote_copy(
        src_ref=src, dst_ref=dst, send_sem=send_sem, recv_sem=recv_sem, device_id=target, device_id_type=MESH
    )


def encode(ref, values):
    block = values.shape[0]
    top = jnp.max(jnp.abs(values), axis=0, keepdims=True)
    power = 14.0 - jnp.floor(jnp.log2(jnp.maximum(top, 1e-30)))
    scaled = jnp.clip(jnp.round(values * jnp.exp2(power)), -32767.0, 32767.0)
    ref[:block] = scaled.astype(jnp.int32).astype(jnp.int16)
    ref[block:] = jnp.broadcast_to(power, (ref.shape[0] - block, LANES)).astype(jnp.int32).astype(jnp.int16)


def decode(ref, block):
    values = ref[:block].astype(jnp.int32).astype(jnp.float32)
    power = ref[block:].astype(jnp.int32).astype(jnp.float32)[:1]
    return values * jnp.exp2(-power)


def kernel(
    feat, stores, slots_per_doc,
    acts, grads, in_basis, grad_basis, lengths, stored, scores,
    acts_v, grads_v, in_basis_v, grad_basis_v, lengths_s, stored_v,
    pair_out, pair_in, line_out, line_in, gathered, wide, queries, sums,
    acts_sem, grads_sem, basis_sem, lengths_sem, stored_sem,
    pair_send, pair_recv, line_send, line_recv, all_send, all_recv, core_send, core_recv,
):
    line = feat // PAIR
    block = acts_v.shape[2]
    docs = block // slots_per_doc
    rank = in_basis.shape[0]
    pairs = rank * rank // LANES
    part_rows = pairs // HALVES
    order = list(range(1, line)) + [0]

    me = lax.axis_index("feat")
    core = lax.axis_index("store")
    my_line, my_pair = me // PAIR, lax.rem(me, PAIR)
    other = 1 - my_pair
    twin = my_line * PAIR + other

    basis_loads = [
        pltpu.make_async_copy(in_basis, in_basis_v, basis_sem.at[0]),
        pltpu.make_async_copy(grad_basis, grad_basis_v, basis_sem.at[1]),
    ]
    for load in basis_loads:
        load.start()
    loads = {}
    for side, half in enumerate((other, my_pair)):
        for step in order:
            spot = lax.rem(my_line + step, line)
            rows = pl.ds(pl.multiple_of((spot * PAIR + half) * block, block), block)
            loads[side, step] = [
                pltpu.make_async_copy(acts.at[rows], acts_v.at[side, step], acts_sem.at[side, step]),
                pltpu.make_async_copy(grads.at[rows], grads_v.at[side, step], grads_sem.at[side, step]),
            ]
    waiting = list(loads.values())

    def start_next():
        if waiting:
            for load in waiting.pop(0):
                load.start()

    for _ in range(AHEAD):
        start_next()

    barrier = pltpu.get_barrier_semaphore()
    for shift in range(1, feat):
        pl.semaphore_signal(barrier, inc=1, device_id={"feat": lax.rem(me + shift, feat)}, device_id_type=MESH)
    for shift in range(1, stores):
        pl.semaphore_signal(barrier, inc=1, device_id={"store": lax.rem(core + shift, stores)}, device_id_type=MESH)

    row = lax.broadcasted_iota(jnp.int32, (rank, LANES), 0)
    lane = lax.broadcasted_iota(jnp.int32, (rank, LANES), 1)
    grad_place = (lane == (row % 2) * (rank // 2) + row // 2).astype(jnp.bfloat16)
    in_place = (lane == row + rank).astype(jnp.bfloat16)
    for load in basis_loads:
        load.wait()
    over_rank = (((0,), (0,)), ((), ()))
    in_wide = lax.dot_general(in_basis_v[...], in_place, over_rank, preferred_element_type=jnp.float32)
    grad_wide = lax.dot_general(grad_basis_v[...], grad_place, over_rank, preferred_element_type=jnp.float32)
    in_wide, grad_wide = in_wide.astype(jnp.bfloat16), grad_wide.astype(jnp.bfloat16)

    def project(side, step):
        for load in loads[side, step]:
            load.wait()
        start_next()
        return jnp.dot(acts_v[side, step], in_wide, preferred_element_type=jnp.float32) + jnp.dot(
            grads_v[side, step], grad_wide, preferred_element_type=jnp.float32
        )

    pair_copies = {}
    for index, step in enumerate(order):
        encode(pair_out.at[step], project(0, step))
        if index == 0:
            pl.semaphore_wait(barrier, feat - 1 + stores - 1)
        pair_copies[step] = remote(
            pair_out.at[step], pair_in.at[step], pair_send.at[step], pair_recv.at[step], {"feat": twin}
        )
        pair_copies[step].start()

    queries[...] = jnp.zeros_like(queries)
    lengths_load = pltpu.make_async_copy(lengths, lengths_s, lengths_sem)
    lengths_load.start()
    half = stored.shape[1] // HALVES
    stored_loads = []
    for part in range(HALVES):
        columns = pl.ds(part * half, half)
        load = pltpu.make_async_copy(stored.at[:, columns], stored_v.at[part], stored_sem.at[part])
        load.start()
        stored_loads.append(load)

    line_copies = {}
    total = None
    for step in order:
        own_half = project(1, step)
        pair_copies[step].wait_recv()
        both = own_half + decode(pair_in.at[step], block)
        if step == 0:
            total = both
        else:
            encode(line_out.at[step], both)
            spot = lax.rem(my_line + step, line)
            line_copies[step] = remote(
                line_out.at[step], line_in.at[step], line_send.at[step], line_recv.at[step],
                {"feat": spot * PAIR + my_pair},
            )
            line_copies[step].start()
    for step in order[:-1]:
        line_copies[step].wait_recv()
        total = total + decode(line_in.at[step], block)

    lengths_load.wait()
    position = lax.broadcasted_iota(jnp.int32, (slots_per_doc, rank), 0)
    left = lax.broadcasted_iota(jnp.int32, (slots_per_doc, LANES), 1) < rank
    for doc in range(docs):
        length = lengths_s[me * docs + doc]
        rows = total[doc * slots_per_doc:(doc + 1) * slots_per_doc]
        grad_side = jnp.where(position < length, rows[:, :rank], 0.0)
        in_side = jnp.where(left, pltpu.roll(rows, rank, 1), rows)
        grad_high, in_high = grad_side.astype(jnp.bfloat16), in_side.astype(jnp.bfloat16)
        grad_low = (grad_side - grad_high.astype(jnp.float32)).astype(jnp.bfloat16)
        in_low = (in_side - in_high.astype(jnp.float32)).astype(jnp.bfloat16)
        outer = lax.dot_general(
            jnp.concatenate([grad_high, grad_high, grad_low]), jnp.concatenate([in_high, in_low, in_high]),
            (((0,), (0,)), ((), ())), preferred_element_type=jnp.float32,
        )
        query = jnp.where(left[:pairs], outer[:pairs], outer[pairs:]) / length.astype(jnp.float32)
        query = query.astype(jnp.bfloat16)
        for part in range(HALVES):
            gathered[part, core, me, pl.ds(doc * part_rows, part_rows), :] = query[part * part_rows:(part + 1) * part_rows]

    sent = []
    for part in range(HALVES):
        own = gathered.at[part, core, me]
        for shift in range(1, feat):
            sent.append(remote(
                own, own, all_send.at[part, shift], all_recv.at[part, shift], {"feat": lax.rem(me + shift, feat)}
            ))
            sent[-1].start()
    core_docs = scores.shape[0] // stores
    span = queries.shape[1] // stores

    def lay_out(part, source, place):
        wide[...] = gathered[part, source].reshape(wide.shape).astype(jnp.float32)
        for pair in range(part_rows):
            queries[part, place * span:place * span + core_docs, pair * LANES:(pair + 1) * LANES] = wide[
                pl.ds(pair, core_docs, part_rows), :
            ].astype(jnp.bfloat16)

    for part in range(HALVES):
        for shift in range(1, feat):
            there = gathered.at[part, core, lax.rem(me + feat - shift, feat)]
            remote(
                there, there, all_send.at[part, shift], all_recv.at[part, shift], {"feat": lax.rem(me + shift, feat)}
            ).wait_recv()
        blocks = gathered.at[part, core]
        for hop in range(1, stores):
            sent.append(remote(
                blocks, blocks, core_send.at[part, hop], core_recv.at[part, hop],
                {"store": lax.rem(core + hop, stores)},
            ))
            sent[-1].start()
        lay_out(part, core, 0)

    tile = 256
    for part in range(HALVES):
        for hop in range(1, stores):
            source = lax.rem(core + stores - hop, stores)
            blocks = gathered.at[part, source]
            remote(
                blocks, blocks, core_send.at[part, hop], core_recv.at[part, hop],
                {"store": lax.rem(core + hop, stores)},
            ).wait_recv()
            lay_out(part, source, hop)
        stored_loads[part].wait()
        for start in range(0, stored.shape[0], tile):
            product = lax.dot_general(
                stored_v[part, start:start + tile, :], queries[part], (((1,), (1,)), ((), ())),
                preferred_element_type=jnp.float32,
            )
            if part:
                product = product + sums[start:start + tile]
            if part + 1 < HALVES:
                sums[start:start + tile] = product
                continue
            turned = product.T
            for hop in range(stores):
                rows = pl.ds(pl.multiple_of(lax.rem(core + stores - hop, stores) * core_docs, core_docs), core_docs)
                scores[rows, start:start + tile] = turned[hop * span:hop * span + core_docs]

    for step in order:
        pair_copies[step].wait_send()
        if step:
            line_copies[step].wait_send()
    for copy in sent:
        copy.wait_send()


def per_device(feat, stores, activations, output_grads, input_basis, grad_basis, lengths, stored_grads):
    tokens, features = activations.shape
    slots_per_doc = tokens // lengths.shape[0]
    rank = input_basis.shape[1]
    rows, depth = stored_grads.shape
    docs = lengths.shape[0] * stores
    padded = -(-docs // LANES) * LANES
    line = feat // PAIR
    block = tokens // feat
    part_rows = rank * rank // LANES // HALVES
    share = block // slots_per_doc * part_rows
    bf16, f32 = jnp.bfloat16, jnp.float32
    dma = pltpu.SemaphoreType.DMA
    anywhere = pl.BlockSpec(memory_space=pl.ANY)
    return pl.pallas_call(
        functools.partial(kernel, feat, stores, slots_per_doc),
        out_shape=pltpu.VMEM((docs, rows), f32),
        in_specs=[anywhere] * 6,
        out_specs=pl.BlockSpec(memory_space=pltpu.VMEM),
        scratch_shapes=[
            pltpu.VMEM((2, line, block, features), bf16),
            pltpu.VMEM((2, line, block, features), bf16),
            pltpu.VMEM((rank, features), bf16),
            pltpu.VMEM((rank, features), bf16),
            pltpu.SMEM(lengths.shape, jnp.int32),
            pltpu.VMEM((HALVES, rows, depth // HALVES), bf16),
            pltpu.VMEM((line, block + HEADER, LANES), jnp.int16),
            pltpu.VMEM((line, block + HEADER, LANES), jnp.int16),
            pltpu.VMEM((line, block + HEADER, LANES), jnp.int16),
            pltpu.VMEM((line, block + HEADER, LANES), jnp.int16),
            pltpu.VMEM((HALVES, stores, feat, share, LANES), bf16),
            pltpu.VMEM((docs // stores * part_rows, LANES), f32),
            pltpu.VMEM((HALVES, padded, depth // HALVES), bf16),
            pltpu.VMEM((rows, padded), f32),
            dma((2, line)), dma((2, line)), dma((2,)), dma(()), dma((HALVES,)),
            dma((line,)), dma((line,)), dma((line,)), dma((line,)),
            dma((HALVES, feat)), dma((HALVES, feat)),
            dma((HALVES, stores)), dma((HALVES, stores)),
        ],
        compiler_params=pltpu.CompilerParams(
            collective_id=0, has_side_effects=True, vmem_limit_bytes=53 * 1024 * 1024
        ),
        cost_estimate=pl.CostEstimate(
            flops=4 * tokens * features * rank + 2 * docs * rows * depth,
            bytes_accessed=4 * tokens * features + 2 * rows * depth + 4 * docs * rows,
            transcendentals=0,
        ),
    )(*[
        pltpu.with_memory_space_constraint(operand, pltpu.HBM)
        for operand in (activations, output_grads, input_basis.T, grad_basis.T, lengths, stored_grads)
    ])


def solution(mesh):
    placed = (
        P(("groups", "store"), "feat"),
        P(("groups", "store"), "feat"),
        P("feat", None),
        P("feat", None),
        P(("groups", "store")),
        P(("groups", "feat", "store"), None),
    )
    return jax.shard_map(
        functools.partial(per_device, mesh.shape["feat"], mesh.shape["store"]),
        mesh=mesh,
        in_specs=placed,
        out_specs=P("groups", ("feat", "store")),
        check_vma=False,
    )
```
